512 devices in a mesh: dp: 8 (over z_lo), pipe: 4 (over x), seq: 16 (over z_hi, y, core).
Axes of the slice: x: 4, y: 4, z: 16 (z_hi: 2, z_lo: 8; z = z_hi * 8 + z_lo), core: 2. Of those that a mesh axis runs over, the one named last changes fastest.
Arguments:
- queries: bfloat16 [4, 8, 2048, 2048], P('pipe', 'dp', 'seq'), may hold values from -6 to 6
- keys: bfloat16 [4, 8, 2048, 512], P('pipe', 'dp', 'seq'), may hold values from -6 to 6
- values: bfloat16 [4, 8, 2048, 512], P('pipe', 'dp', 'seq'), may hold values from -6 to 6
- grad_next: bfloat16 [4, 8, 2048, 2048], P('pipe', 'dp', 'seq'), may hold values from -6 to 6
- normed: bfloat16 [4, 8, 2048, 4096], P('pipe', 'dp', 'seq'), may hold values from -6 to 6
- value_weight: bfloat16 [4, 4096, 512], P('pipe', 'seq'), may hold values from -0.09375 to 0.09375
Outputs:
- grad_queries: bfloat16 [4, 8, 2048, 2048], P('pipe', 'dp', 'seq')
- grad_keys: bfloat16 [4, 8, 2048, 512], P('pipe', 'dp', 'seq')
- grad_normed: bfloat16 [4, 8, 2048, 4096], P('pipe', 'dp', 'seq')
- grad_value_weight: float32 [4, 4096, 512], P('pipe', 'seq')
The draws below stay inside these ranges and needn't reach their ends.
All inputs are finite; a program needn't handle non-finite values.
Results may differ from the reference program's by a relative error of at most 0.019.
Values may be sent and summed in bfloat16 or wider, within the bound.
A program may use at most 64 MiB of HBM per device.

```python
import jax
import jax.numpy as jnp
from jax import lax

D = 4096
HEAD = 128
HQ = 16
KV = 4
SECTIONS = 4
SEQS = 8
LENGTH = 2048


def draw_queries(key, part):
    shape = (SECTIONS, SEQS, LENGTH, KV, HQ // KV, HEAD)
    base = jnp.clip(jax.random.normal(jax.random.fold_in(key, 1), shape, jnp.float32), -4.0, 4.0)
    return base.reshape(SECTIONS, SEQS, LENGTH, HQ * HEAD).astype(jnp.bfloat16)


def draw_keys(key, part):
    shape = (SECTIONS, SEQS, LENGTH, KV, 1, HEAD)
    base = jnp.clip(jax.random.normal(jax.random.fold_in(key, 2), shape, jnp.float32), -4.0, 4.0)
    return base.reshape(SECTIONS, SEQS, LENGTH, KV * HEAD).astype(jnp.bfloat16)


def level_of(stream_key, dims, shards, smallest, high):
    level = 1.0
    for axis_at, shards_of in shards:
        draws = jax.random.uniform(jax.random.fold_in(jax.random.fold_in(stream_key, 6), axis_at), (shards_of,), jnp.float32, smallest / len(shards), high / len(shards))
        level = level * jnp.repeat(jnp.exp(draws), dims[axis_at] // shards_of).reshape((-1,) + (1,) * (len(dims) - 1 - axis_at))
    return level


def noise(own_key, shape, scale, most, pieces=(), kind=jnp.bfloat16):
    result = scale * jax.random.normal(own_key, shape, jnp.float32)
    if pieces:
        result = result * level_of(own_key, shape, pieces, -0.22, 0.18)
    return jnp.clip(result, -most, most).astype(kind)


def setup_inputs(seed: int = 0) -> dict:
    seeds = jax.random.split(jax.random.key(seed), 7)
    return {
        "queries": draw_queries(jax.random.fold_in(seeds[6], 71), 0),
        "keys": draw_keys(jax.random.fold_in(seeds[6], 71), 0),
        "values": noise(seeds[2], (SECTIONS, SEQS, LENGTH, KV * HEAD), 1.0, 6.0, ((0, 4), (1, 8), (2, 16))),
        "grad_next": noise(seeds[3], (SECTIONS, SEQS, LENGTH, HQ * HEAD), 1.0, 6.0, ((0, 4), (1, 8), (2, 16))),
        "normed": noise(seeds[4], (SECTIONS, SEQS, LENGTH, D), 1.0, 6.0, ((0, 4), (1, 8), (2, 16))),
        "value_weight": noise(seeds[5], (SECTIONS, D, KV * HEAD), D ** -0.5, 0.09375, ((0, 4), (1, 16))),
    }


masked_value = -1e30


def attend(query_head, key_head, value_head, upstream_head):
    length = query_head.shape[0]
    block_rows = min(512, length)
    factor = HEAD ** -0.5
    query_parts = []
    grad_key = jnp.zeros((length, HEAD), jnp.float32)
    grad_value = jnp.zeros((length, HEAD), jnp.float32)
    for block_index in range(length // block_rows):
        first_row = block_index * block_rows
        finish = first_row + block_rows
        query_block = query_head[first_row:finish]
        upstream_block = upstream_head[first_row:finish]
        key_prefix = key_head[:finish]
        value_prefix = value_head[:finish]
        scores = lax.dot_general(query_block, key_prefix, (((1,), (1,)), ((), ())), preferred_element_type=jnp.float32) * factor
        row_pos = first_row + jnp.arange(block_rows, dtype=jnp.int32)[:, None]
        col_pos = jnp.arange(finish, dtype=jnp.int32)[None, :]
        scores = jnp.where(col_pos <= row_pos, scores, masked_value)
        shifted = jnp.exp(scores - jnp.max(scores, axis=1, keepdims=True))
        softmax_rows = shifted / jnp.sum(shifted, axis=1, keepdims=True)
        probs_half = softmax_rows.astype(jnp.bfloat16)
        attn_out = jnp.dot(probs_half, value_prefix, preferred_element_type=jnp.float32)
        row_delta = jnp.sum(upstream_block.astype(jnp.float32) * attn_out, axis=1, keepdims=True)
        grad_probs = lax.dot_general(upstream_block, value_prefix, (((1,), (1,)), ((), ())), preferred_element_type=jnp.float32)
        grad_scores = (softmax_rows * (grad_probs - row_delta)).astype(jnp.bfloat16)
        query_parts.append(jnp.dot(grad_scores, key_prefix, preferred_element_type=jnp.float32) * factor)
        key_part = lax.dot_general(grad_scores, query_block, (((0,), (0,)), ((), ())), preferred_element_type=jnp.float32) * factor
        value_part = lax.dot_general(probs_half, upstream_block, (((0,), (0,)), ((), ())), preferred_element_type=jnp.float32)
        grad_key = grad_key.at[:finish].add(key_part)
        grad_value = grad_value.at[:finish].add(value_part)
    return jnp.concatenate(query_parts, axis=0), grad_key, grad_value


def reference(queries, keys, values, grad_next, normed, value_weight):
    upstream = jnp.roll(grad_next, -1, axis=0)
    repeats = HQ // KV

    def heads_of(source, head_count):
        return source.reshape(SECTIONS * SEQS, LENGTH, head_count, HEAD).transpose(0, 2, 1, 3)

    def tokens_of(source, head_count):
        return source.reshape(SECTIONS, SEQS, head_count, LENGTH, HEAD).transpose(0, 1, 3, 2, 4).reshape(SECTIONS, SEQS, LENGTH, head_count * HEAD)

    query_heads = heads_of(queries, HQ).reshape(-1, LENGTH, HEAD)
    key_heads = jnp.repeat(heads_of(keys, KV), repeats, axis=1).reshape(-1, LENGTH, HEAD)
    value_heads = jnp.repeat(heads_of(values, KV), repeats, axis=1).reshape(-1, LENGTH, HEAD)
    upstream_heads = heads_of(upstream, HQ).reshape(-1, LENGTH, HEAD)
    grad_query, grad_key, grad_value = lax.map(lambda operands: attend(*operands), (query_heads, key_heads, value_heads, upstream_heads))
    grad_queries = tokens_of(grad_query.astype(jnp.bfloat16), HQ)

    def grouped(head_terms):
        rounded = lax.optimization_barrier(head_terms.astype(jnp.bfloat16)).astype(jnp.float32)
        return rounded.reshape(SECTIONS * SEQS, KV, repeats, LENGTH, HEAD).sum(axis=2).astype(jnp.bfloat16)

    grad_keys = tokens_of(grouped(grad_key), KV)
    grad_values = tokens_of(grouped(grad_value), KV)
    grad_normed = jnp.einsum("sbtk,sdk->sbtd", grad_values.astype(jnp.float32), value_weight.astype(jnp.float32)).astype(jnp.bfloat16)
    grad_value_weight = jnp.einsum("sbtd,sbtk->sdk", normed.astype(jnp.float32), grad_values.astype(jnp.float32))
    return (grad_queries, grad_keys, grad_normed, grad_value_weight)
```

```python
import functools

import jax
import jax.numpy as jnp
from jax import lax
from jax.experimental import pallas as pl
from jax.experimental.pallas import tpu as pltpu
from jax.sharding import PartitionSpec as P

HEAD = 128
HQ = 16
CHUNK = 256
GROUP = 512
FACTOR = HEAD**-0.5
LOG2E = 1.4426950408889634
MASKED = -1e30
MESH = pl.DeviceIdType.MESH
F32 = jnp.float32
BF16 = jnp.bfloat16


def nt(a, b):
    return lax.dot_general(a, b, (((1,), (1,)), ((), ())), preferred_element_type=F32)


def nn(a, b):
    return lax.dot_general(a, b, (((1,), (0,)), ((), ())), preferred_element_type=F32)


def tn(a, b):
    return lax.dot_general(a, b, (((0,), (0,)), ((), ())), preferred_element_type=F32)


def aligned(index, size):
    return pl.ds(pl.multiple_of(index * size, size), size)


def fold8(x, op):
    return op(x.reshape(CHUNK // 8, 8, GROUP), axis=0)


def kernel(
    q_ref,
    k_ref,
    v_ref,
    g_ref,
    n_ref,
    w_ref,
    dq_o,
    dk_o,
    gn_o,
    dw_o,
    kbuf,
    vbuf,
    qbuf,
    ubuf,
    nbuf,
    wbuf,
    sbuf,
    ebuf,
    qs,
    us,
    stat,
    dvsend,
    dvown,
    dvsib,
    dvcs,
    dvcr,
    dksend,
    dkown,
    dksib,
    dkcs,
    dkcr,
    dvfull,
    dkfin,
    dqs,
    rsend,
    rown,
    rsib,
    rfull,
    zrecv,
    zfin,
    gns,
    send_sems,
    recv_sems,
):
    i = lax.axis_index("dp")
    x = lax.axis_index("pipe")
    s = lax.axis_index("seq")
    h = s // 8
    y = lax.rem(s // 2, 4)
    c = lax.rem(s, 2)
    z = h * 8 + i
    lower = h == 0
    upper = h == 1
    used = [0]
    started = []

    def rc(src, dst, dev):
        n = used[0]
        used[0] += 1
        return pltpu.make_async_remote_copy(
            src_ref=src,
            dst_ref=dst,
            send_sem=send_sems.at[n],
            recv_sem=recv_sems.at[n],
            device_id=dev,
            device_id_type=MESH,
        )

    def go(copy):
        copy.start()
        started.append(copy)

    def ydev(d):
        return {"seq": h * 8 + lax.rem(y + d, 4) * 2 + c}

    def zdev(d):
        t = lax.rem(z + d, 16)
        return {"dp": lax.rem(t, 8), "seq": (t // 8) * 8 + y * 2 + c}

    sib = {"seq": s + 1 - 2 * c}
    ys = [lax.rem(y + d, 4) for d in range(4)]
    yfrom = [lax.rem(y + 4 - d, 4) for d in range(4)]

    bar = pltpu.get_barrier_semaphore()
    count = 0
    for d in range(1, 4):
        pl.semaphore_signal(bar, inc=1, device_id=ydev(d), device_id_type=MESH)
        count += 1
    for d in range(4):
        pl.semaphore_signal(
            bar,
            inc=1,
            device_id={"pipe": lax.rem(x + 1, 4), "seq": ydev(d)["seq"]},
            device_id_type=MESH,
        )
        count += 1
    pl.semaphore_signal(bar, inc=1, device_id=sib, device_id_type=MESH)
    count += 1
    for d in range(1, 16):
        pl.semaphore_signal(bar, inc=1, device_id=zdev(d), device_id_type=MESH)
        count += 1
    pl.semaphore_wait(bar, count)

    my_rows = aligned(y, 128)
    kc = [
        rc(k_ref.at[:, aligned(ys[d], 128)], kbuf.at[0, c, my_rows], ydev(d)) for d in range(1, 4)
    ]
    for copy in kc:
        go(copy)
    kbuf[0, c, my_rows, :] = k_ref[:, my_rows]

    def crossing(buf):
        return [
            rc(buf.at[0, c, aligned(yfrom[d], 128)], buf.at[1, c, aligned(yfrom[d], 128)], zdev(8))
            for d in range(4)
        ]

    kx = crossing(kbuf)

    @pl.when(lower)
    def _():
        kx[0].start()

    qc = [
        rc(q_ref.at[:, aligned(ys[d], GROUP)], qbuf.at[y], ydev(d)) for d in range(1, 4)
    ]
    for copy in qc:
        go(copy)
    qbuf[y] = q_ref[:, aligned(y, GROUP)]
    vc = [
        rc(v_ref.at[:, aligned(ys[d], 128)], vbuf.at[0, c, my_rows], ydev(d)) for d in range(1, 4)
    ]
    for copy in vc:
        go(copy)
    vbuf[0, c, my_rows, :] = v_ref[:, my_rows]
    vx = crossing(vbuf)
    uc = [
        rc(
            g_ref.at[:, aligned(ys[d], GROUP)],
            ubuf.at[y],
            {"pipe": lax.rem(x + 3, 4), "seq": ydev(d)["seq"]},
        )
        for d in range(4)
    ]
    for copy in uc:
        go(copy)

    for d in range(1, 4):
        kc[d - 1].wait_recv()

        @pl.when(lower)
        def _():
            kx[d].start()

    ksib = rc(kbuf.at[0, c], kbuf.at[0, c], sib)
    go(ksib)
    for d in range(1, 4):
        qc[d - 1].wait_recv()
    for b in range(4):
        for hd in range(4):
            qs[b, hd * 128 : hd * 128 + 128, :] = qbuf[b, :, hd * 128 : hd * 128 + 128]

    @pl.when(lower)
    def _():
        vx[0].start()

    for d in range(1, 4):
        vc[d - 1].wait_recv()

        @pl.when(lower)
        def _():
            vx[d].start()

    vsib = rc(vbuf.at[0, c], vbuf.at[0, c], sib)
    go(vsib)

    wsib = rc(w_ref, wbuf.at[0, c], sib)
    go(wsib)
    wbuf[0, c] = w_ref[...]
    n = used[0]
    used[0] += 2

    def wcopy(src, which, d):
        return pltpu.make_async_remote_copy(
            src_ref=src,
            dst_ref=wbuf.at[1, c],
            send_sem=send_sems.at[n + which],
            recv_sem=recv_sems.at[n],
            device_id=zdev(d),
            device_id_type=MESH,
        )

    first_up = i == 7
    first_down = i == 0
    w_first = [wcopy(w_ref, 0, 15), wcopy(w_ref, 0, 1)]
    w_next = [wcopy(wbuf.at[1, c], 1, 1), wcopy(wbuf.at[1, c], 1, 15)]

    @pl.when(first_down)
    def _():
        w_first[0].start()

    @pl.when(first_up)
    def _():
        w_first[1].start()

    def forward_w(step):
        @pl.when(i == step)
        def _():
            w_first[0].wait_recv()
            w_next[0].start()

        @pl.when(i == 7 - step)
        def _():
            w_first[0].wait_recv()
            w_next[1].start()

    ksib.wait_recv()

    def kchunk(buf, half, j):
        rows = aligned(j, 128)
        return jnp.concatenate([buf[half, 0, rows, :], buf[half, 1, rows, :]], axis=0)

    for b in range(4):

        def body(j, top):
            sc = nt(kchunk(kbuf, 0, j), qs[b])
            sbuf[b, aligned(j, CHUNK), :] = sc
            return jnp.maximum(top, fold8(sc, jnp.max))

        top = lax.fori_loop(0, b, body, jnp.full((8, GROUP), MASKED, F32))
        sc = nt(kchunk(kbuf, 0, b), qs[b])
        key_pos = lax.broadcasted_iota(jnp.int32, (CHUNK, GROUP), 0)
        row_pos = lax.rem(lax.broadcasted_iota(jnp.int32, (CHUNK, GROUP), 1), 128) + c * 128
        sc = jnp.where(key_pos <= row_pos, sc, MASKED)
        sbuf[b, b * CHUNK : (b + 1) * CHUNK, :] = sc
        stat[b] = jnp.maximum(top, fold8(sc, jnp.max))

    for d in range(4):
        uc[d].wait_recv()
    nc = [
        rc(
            n_ref.at[:, aligned((h + r * (1 - 2 * h)) * 4 + ys[d], GROUP)],
            nbuf.at[r, my_rows],
            ydev(d),
        )
        for d in range(1, 4)
        for r in range(2)
    ]
    for copy in nc:
        go(copy)
    for r in range(2):
        nbuf[r, my_rows, :] = n_ref[:, aligned((h + r * (1 - 2 * h)) * 4 + y, GROUP)]
    vsib.wait_recv()
    forward_w(0)

    kxs = rc(kbuf.at[1, c], kbuf.at[1, c], sib)
    vxs = rc(vbuf.at[1, c], vbuf.at[1, c], sib)

    @pl.when(upper)
    def _():
        for d in range(4):
            kx[d].wait_recv()
        kxs.start()
        kxs.wait_recv()
        for b in range(4):

            def body(j, top):
                sc = nt(kchunk(kbuf, 1, j), qs[b])
                sbuf[b, aligned(j + 4, CHUNK), :] = sc
                return jnp.maximum(top, fold8(sc, jnp.max))

            stat[b] = lax.fori_loop(0, 4, body, stat[b])

    for b in range(4):
        shift = jnp.max(stat[b], axis=0, keepdims=True) * (FACTOR * LOG2E)

        def body(j, total):
            e = jnp.exp2(sbuf[b, aligned(j, CHUNK), :] * (FACTOR * LOG2E) - shift)
            ebuf[b, aligned(j, CHUNK), :] = e.astype(BF16)
            return total + fold8(e, jnp.sum)

        total = lax.fori_loop(0, b + 1, body, jnp.zeros((8, GROUP), F32))
        total = lax.fori_loop(4, 4 + 4 * h, body, total)
        inverse = 1.0 / jnp.sum(total, axis=0, keepdims=True)
        stat[b] = jnp.broadcast_to(inverse, (8, GROUP))
        for hd in range(4):
            cols = slice(hd * 128, hd * 128 + 128)
            spread = jnp.broadcast_to(inverse[:, cols], (128, 128)).T
            us[b, cols, :] = (ubuf[b, :, cols].astype(F32) * spread).astype(BF16)

    def split(term, own, send, rows):
        first, second = term[:128], term[128:]
        own[rows, :] = jnp.where(c == 0, first, second)
        send[rows, :] = jnp.where(c == 0, second, first).astype(BF16)

    def remote_terms(right, own, send):
        def body(j, carry):
            term = nn(ebuf[0, aligned(j + 4, CHUNK), :], right[0])
            for b in range(1, 4):
                term += nn(ebuf[b, aligned(j + 4, CHUNK), :], right[b])
            split(term, own, send, aligned(j, 128))
            return carry

        lax.fori_loop(0, 4, body, 0)

    def own_terms(right, own, send):
        for j in range(4):
            term = nn(ebuf[j, j * CHUNK : (j + 1) * CHUNK, :], right[j])
            for b in range(j + 1, 4):
                term += nn(ebuf[b, j * CHUNK : (j + 1) * CHUNK, :], right[b])
            split(term, own, send, slice(j * 128, j * 128 + 128))

    dvxs = rc(dvsend.at[1], dvsib.at[1], sib)
    dvos = rc(dvsend.at[0], dvsib.at[0], sib)
    dvx = rc(dvcs, dvcr, zdev(8))

    @pl.when(upper)
    def _():
        remote_terms(us, dvown.at[1], dvsend.at[1])
        dvxs.start()

    own_terms(us, dvown.at[0], dvsend.at[0])
    go(dvos)
    forward_w(1)

    @pl.when(upper)
    def _():
        dvxs.wait_recv()
        dvcs[...] = (dvown[1] + dvsib[1].astype(F32)).astype(BF16)
        dvx.start()

    my_head = aligned(y, 128)
    dvb = [rc(dvfull.at[:, my_head], dvfull.at[:, my_head], ydev(d)) for d in range(1, 4)]

    def send_dv():
        for copy in dvb:
            copy.start()

    dvos.wait_recv()

    @pl.when(upper)
    def _():
        dvfull[:, my_head] = (dvown[0] + dvsib[0].astype(F32)).astype(BF16)
        send_dv()
        for d in range(4):
            vx[d].wait_recv()
        vxs.start()
        vxs.wait_recv()

    for b in range(4):

        def body(j, total):
            half = j // 4
            dp = nt(kchunk(vbuf, half, lax.rem(j, 4)), us[b])
            t = ebuf[b, aligned(j, CHUNK), :].astype(F32) * dp
            sbuf[b, aligned(j, CHUNK), :] = t
            return total + fold8(t, jnp.sum)

        total = lax.fori_loop(0, b + 1, body, jnp.zeros((8, GROUP), F32))
        total = lax.fori_loop(4, 4 + 4 * h, body, total)
        inverse = stat[b]
        delta = jnp.sum(total, axis=0, keepdims=True) * inverse[0:1]

        def grads(j, carry):
            e = ebuf[b, aligned(j, CHUNK), :].astype(F32)
            ebuf[b, aligned(j, CHUNK), :] = (sbuf[b, aligned(j, CHUNK), :] - e * delta).astype(BF16)
            return carry

        lax.fori_loop(0, b + 1, grads, 0)
        lax.fori_loop(4, 4 + 4 * h, grads, 0)

    dkxs = rc(dksend.at[1], dksib.at[1], sib)
    dkos = rc(dksend.at[0], dksib.at[0], sib)
    dkx = rc(dkcs, dkcr, zdev(8))

    @pl.when(upper)
    def _():
        remote_terms(qs, dkown.at[1], dksend.at[1])
        dkxs.start()

    own_terms(qs, dkown.at[0], dksend.at[0])
    go(dkos)

    @pl.when(upper)
    def _():
        dkxs.wait_recv()
        dkcs[...] = ((dkown[1] + dksib[1].astype(F32)) * FACTOR).astype(BF16)
        dkx.start()

    forward_w(2)

    for b in range(4):

        def body(j, total):
            return total + tn(
                kchunk(kbuf, j // 4, lax.rem(j, 4)), ebuf[b, aligned(j, CHUNK), :]
            )

        total = lax.fori_loop(0, b + 1, body, jnp.zeros((HEAD, GROUP), F32))
        total = lax.fori_loop(4, 4 + 4 * h, body, total)
        total = total * FACTOR
        for hd in range(4):
            cols = slice(hd * 128, hd * 128 + 128)
            dqs[b, :, cols] = total[:, cols].T.astype(BF16)
    my_group = aligned(y, GROUP)
    dqc = [rc(dqs.at[ys[d]], dq_o.at[:, my_group], ydev(d)) for d in range(1, 4)]
    for copy in dqc:
        go(copy)
    dq_o[:, my_group] = dqs[y]

    dkos.wait_recv()
    dkc = [
        rc(dkfin.at[aligned(ys[d], 128)], dk_o.at[:, my_head], ydev(d)) for d in range(1, 4)
    ]

    def send_dk():
        for copy in dkc:
            copy.start()
        dk_o[:, my_head] = dkfin[my_rows, :]

    @pl.when(upper)
    def _():
        dkfin[...] = ((dkown[0] + dksib[0].astype(F32)) * FACTOR).astype(BF16)
        send_dk()

    @pl.when(lower)
    def _():
        dvx.wait_recv()
        dvfull[:, my_head] = (
            dvown[0] + dvsib[0].astype(F32) + dvcr[...].astype(F32)
        ).astype(BF16)
        send_dv()

    @pl.when(jnp.logical_or(i == 3, i == 4))
    def _():
        w_first[0].wait_recv()

    ws2 = rc(wbuf.at[1, c], wbuf.at[1, c], sib)
    go(ws2)
    for copy in nc:
        copy.wait_recv()
    for copy in dvb:
        copy.wait_recv()

    for r in range(2):
        rsend[r] = tn(nbuf[r, :, aligned(1 - c, CHUNK)], dvfull[...]).astype(BF16)
    rs = rc(rsend, rsib, sib)
    go(rs)
    for r in range(2):
        rown[r] = tn(nbuf[r, :, aligned(c, CHUNK)], dvfull[...])
    rs.wait_recv()
    for r in range(2):
        rfull[r] = (rown[r] + rsib[r].astype(F32)).astype(BF16)
    zc = []
    for d in range(1, 16):
        t = lax.rem(z + d, 16)
        r = lax.rem(t // 8 + h, 2)
        copy = rc(rfull.at[r, aligned(lax.rem(t, 8), 32)], zrecv.at[d - 1], zdev(d))
        zc.append(copy)
        go(copy)

    wsib.wait_recv()
    ws2.wait_recv()
    for r in range(2):
        for cc in range(2):
            gns[r, :, cc * CHUNK : (cc + 1) * CHUNK] = nt(dvfull[...], wbuf[r, cc]).astype(BF16)
    gc = []
    for r in range(2):
        cols = aligned((h + r * (1 - 2 * h)) * 4 + y, GROUP)
        for d in range(1, 4):
            copy = rc(gns.at[r, aligned(ys[d], 128)], gn_o.at[:, cols], ydev(d))
            gc.append(copy)
            go(copy)
        gn_o[:, cols] = gns[r, my_rows, :]

    @pl.when(lower)
    def _():
        dkx.wait_recv()
        dkfin[...] = (
            (dkown[0] + dksib[0].astype(F32)) * FACTOR + dkcr[...].astype(F32)
        ).astype(BF16)
        send_dk()

    my_piece = aligned(i, 32)
    total = rfull[0, my_piece, :].astype(F32)
    for d in range(15):
        zc[d].wait_recv()
        total += zrecv[d].astype(F32)
    zfin[my_piece, :] = total.astype(BF16)
    pc = [
        rc(zfin.at[my_piece], zfin.at[my_piece], {"dp": lax.rem(i + d, 8)}) for d in range(1, 8)
    ]
    for copy in pc:
        go(copy)
    for copy in pc:
        copy.wait_recv()
    dw_o[...] = zfin[...].astype(F32)

    for copy in dqc + dkc + gc:
        copy.wait_recv()
    for copy in started + dvb + dkc:
        copy.wait_send()

    @pl.when(lower)
    def _():
        for copy in kx + vx:
            copy.wait_send()

    @pl.when(upper)
    def _():
        for copy in [kxs, vxs, dvxs, dvx, dkxs, dkx]:
            copy.wait_send()

    @pl.when(jnp.logical_or(first_up, first_down))
    def _():
        w_first[0].wait_send()

    @pl.when(jnp.logical_and(i != 3, i != 4))
    def _():
        w_next[0].wait_send()


def local(queries, keys, values, grad_next, normed, value_weight):
    vmem = pl.BlockSpec(memory_space=pltpu.VMEM)

    def buf(*shape, dtype=BF16):
        return pltpu.VMEM(shape, dtype)

    count = 100
    dq, dk, gn, dw = pl.pallas_call(
        kernel,
        out_shape=(
            jax.ShapeDtypeStruct((128, 2048), BF16),
            jax.ShapeDtypeStruct((128, 512), BF16),
            jax.ShapeDtypeStruct((128, 4096), BF16),
            jax.ShapeDtypeStruct((256, 512), F32),
        ),
        in_specs=[vmem] * 6,
        out_specs=(vmem,) * 4,
        scratch_shapes=[
            buf(2, 2, 512, 128),
            buf(2, 2, 512, 128),
            buf(4, 128, GROUP),
            buf(4, 128, GROUP),
            buf(2, 512, GROUP),
            buf(2, 2, 256, 512),
            buf(4, 2048, GROUP, dtype=F32),
            buf(4, 2048, GROUP),
            buf(4, GROUP, HEAD),
            buf(4, GROUP, HEAD),
            buf(4, 8, GROUP, dtype=F32),
            buf(2, 512, 128),
            buf(2, 512, 128, dtype=F32),
            buf(2, 512, 128),
            buf(512, 128),
            buf(512, 128),
            buf(2, 512, 128),
            buf(2, 512, 128, dtype=F32),
            buf(2, 512, 128),
            buf(512, 128),
            buf(512, 128),
            buf(512, 512),
            buf(512, 128),
            buf(4, 128, GROUP),
            buf(2, 256, 512),
            buf(2, 256, 512, dtype=F32),
            buf(2, 256, 512),
            buf(2, 256, 512),
            buf(15, 32, 512),
            buf(256, 512),
            buf(2, 512, GROUP),
            pltpu.SemaphoreType.DMA((count,)),
            pltpu.SemaphoreType.DMA((count,)),
        ],
        compiler_params=pltpu.CompilerParams(
            collective_id=0, has_side_effects=True, vmem_limit_bytes=52 * 1024 * 1024
        ),
        cost_estimate=pl.CostEstimate(
            flops=6_000_000_000, bytes_accessed=5_000_000, transcendentals=3_000_000
        ),
    )(queries[0, 0], keys[0, 0], values[0, 0], grad_next[0, 0], normed[0, 0], value_weight[0])
    return dq[None, None], dk[None, None], gn[None, None], dw[None]


def solution(mesh):
    placed = (
        P("pipe", "dp", "seq", None),
        P("pipe", "dp", "seq", None),
        P("pipe", "dp", "seq", None),
        P("pipe", "dp", "seq", None),
        P("pipe", "dp", "seq", None),
        P("pipe", "seq", None),
    )
    return jax.shard_map(
        local,
        mesh=mesh,
        in_specs=placed,
        out_specs=(
            P("pipe", "dp", "seq", None),
            P("pipe", "dp", "seq", None),
            P("pipe", "dp", "seq", None),
            P("pipe", "seq", None),
        ),
        check_vma=False,
    )
```

```python
import functools

import jax
import jax.numpy as jnp
from jax import lax
from jax.experimental import pallas as pl
from jax.experimental.pallas import tpu as pltpu
from jax.sharding import PartitionSpec as P

HEAD = 128
HQ = 16
CHUNK = 256
GROUP = 512
FACTOR = HEAD**-0.5
LOG2E = 1.4426950408889634
MASKED = -1e30
MESH = pl.DeviceIdType.MESH
F32 = jnp.float32
BF16 = jnp.bfloat16


def nt(a, b):
    return lax.dot_general(a, b, (((1,), (1,)), ((), ())), preferred_element_type=F32)


def nn(a, b):
    return lax.dot_general(a, b, (((1,), (0,)), ((), ())), preferred_element_type=F32)


def tn(a, b):
    return lax.dot_general(a, b, (((0,), (0,)), ((), ())), preferred_element_type=F32)


def aligned(index, size):
    return pl.ds(pl.multiple_of(index * size, size), size)


def fold8(x, op):
    return op(x.reshape(CHUNK // 8, 8, GROUP), axis=0)


def kernel(
    q_ref,
    k_ref,
    v_ref,
    g_ref,
    n_ref,
    w_ref,
    dq_o,
    dk_o,
    gn_o,
    dw_o,
    kbuf,
    vbuf,
    qbuf,
    ubuf,
    nbuf,
    wbuf,
    sbuf,
    ebuf,
    qs,
    ust,
    kt,
    vt,
    stat,
    dvsend,
    dvown,
    dvsib,
    dvcs,
    dvcr,
    dksend,
    dkown,
    dksib,
    dkcs,
    dkcr,
    dvfull,
    dkfin,
    dqs,
    rsend,
    rsib,
    rfull,
    z1recv,
    tfull,
    z2recv,
    zfin,
    gns,
    send_sems,
    recv_sems,
    local_sems,
):
    i = lax.axis_index("dp")
    x = lax.axis_index("pipe")
    s = lax.axis_index("seq")
    h = s // 8
    y = lax.rem(s // 2, 4)
    c = lax.rem(s, 2)
    z = h * 8 + i
    lower = h == 0
    upper = h == 1
    used = [0]
    local_used = [0]
    started = []

    def lc(src, dst):
        n = local_used[0]
        local_used[0] += 1
        return pltpu.make_async_copy(src, dst, local_sems.at[n])

    def rc(src, dst, dev):
        n = used[0]
        used[0] += 1
        return pltpu.make_async_remote_copy(
            src_ref=src,
            dst_ref=dst,
            send_sem=send_sems.at[n],
            recv_sem=recv_sems.at[n],
            device_id=dev,
            device_id_type=MESH,
        )

    def go(copy):
        copy.start()
        started.append(copy)

    def ydev(d):
        return {"seq": h * 8 + lax.rem(y + d, 4) * 2 + c}

    def zdev(d):
        t = lax.rem(z + d, 16)
        return {"dp": lax.rem(t, 8), "seq": (t // 8) * 8 + y * 2 + c}

    sib = {"seq": s + 1 - 2 * c}
    ys = [lax.rem(y + d, 4) for d in range(4)]
    yfrom = [lax.rem(y + 4 - d, 4) for d in range(4)]

    bar = pltpu.get_barrier_semaphore()
    count = 0
    for d in range(1, 4):
        pl.semaphore_signal(bar, inc=1, device_id=ydev(d), device_id_type=MESH)
        count += 1
    for d in range(4):
        pl.semaphore_signal(
            bar,
            inc=1,
            device_id={"pipe": lax.rem(x + 1, 4), "seq": ydev(d)["seq"]},
            device_id_type=MESH,
        )
        count += 1
    pl.semaphore_signal(bar, inc=1, device_id=sib, device_id_type=MESH)
    count += 1
    for d in range(1, 8):
        dev = {"dp": lax.rem(i + d, 8)}
        pl.semaphore_signal(bar, inc=1, device_id=dev, device_id_type=MESH)
        count += 1
    for d in (1, 4, 8, 12, 15):
        pl.semaphore_signal(bar, inc=1, device_id=zdev(d), device_id_type=MESH)
        count += 1
    my_rows = aligned(y, 128)
    my_group = aligned(y, GROUP)
    column_blocks = [lax.rem(h + r, 2) * 4 for r in range(2)]
    own_k = lc(k_ref.at[:, my_rows], kbuf.at[0, c, my_rows])
    own_q = lc(q_ref.at[:, my_group], qbuf.at[y])
    own_v = lc(v_ref.at[:, my_rows], vbuf.at[0, c, my_rows])
    own_w = lc(w_ref, wbuf.at[0, c])
    own_n = [
        lc(n_ref.at[:, aligned(column_blocks[r] + y, GROUP)], nbuf.at[r, my_rows])
        for r in range(2)
    ]
    for copy in [own_k, own_q, own_v, own_w] + own_n:
        copy.start()
    pl.semaphore_wait(bar, count)

    kc = [
        rc(k_ref.at[:, aligned(ys[d], 128)], kbuf.at[0, c, my_rows], ydev(d)) for d in range(1, 4)
    ]
    for copy in kc:
        go(copy)

    def crossing(ref, buf):
        copies = []
        for d in range(4):
            rows = aligned(yfrom[d], 128)
            src = ref.at[:, my_rows] if d == 0 else buf.at[0, c, rows]
            copies.append(rc(src, buf.at[1, c, rows], zdev(8)))
        return copies

    kx = crossing(k_ref, kbuf)

    @pl.when(lower)
    def _():
        kx[0].start()

    qc = [
        rc(q_ref.at[:, aligned(ys[d], GROUP)], qbuf.at[y], ydev(d)) for d in range(1, 4)
    ]
    for copy in qc:
        go(copy)
    vx = crossing(v_ref, vbuf)
    uc = [
        rc(
            g_ref.at[:, aligned(ys[d], GROUP)],
            ubuf.at[y],
            {"pipe": lax.rem(x + 3, 4), "seq": ydev(d)["seq"]},
        )
        for d in range(4)
    ]
    for copy in uc:
        go(copy)

    for d in range(1, 4):
        kc[d - 1].wait_recv()

        @pl.when(lower)
        def _():
            kx[d].start()

    own_k.wait()
    ksib = rc(kbuf.at[0, c], kbuf.at[0, c], sib)
    go(ksib)
    for d in range(1, 4):
        qc[d - 1].wait_recv()
    own_q.wait()
    vc = [
        rc(v_ref.at[:, aligned(ys[d], 128)], vbuf.at[0, c, my_rows], ydev(d)) for d in range(1, 4)
    ]
    for copy in vc:
        go(copy)
    for b in range(4):
        for hd in range(4):
            qs[b, hd * 128 : hd * 128 + 128, :] = qbuf[b, :, hd * 128 : hd * 128 + 128]


    wsib = rc(w_ref, wbuf.at[0, c], sib)
    go(wsib)
    n = used[0]
    used[0] += 2

    def wcopy(src, which, d):
        return pltpu.make_async_remote_copy(
            src_ref=src,
            dst_ref=wbuf.at[1, c],
            send_sem=send_sems.at[n + which],
            recv_sem=recv_sems.at[n],
            device_id=zdev(d),
            device_id_type=MESH,
        )

    first_up = i == 7
    first_down = i == 0

    def start_w():
        @pl.when(first_down)
        def _():
            w_first[0].start()

        @pl.when(first_up)
        def _():
            w_first[1].start()

    w_first = [wcopy(w_ref, 0, 15), wcopy(w_ref, 0, 1)]
    w_next = [wcopy(wbuf.at[1, c], 1, 1), wcopy(wbuf.at[1, c], 1, 15)]

    @pl.when(upper)
    def _():
        start_w()

    def forward_w(half, step):
        @pl.when(jnp.logical_and(half, i == step))
        def _():
            w_first[0].wait_recv()
            w_next[0].start()

        @pl.when(jnp.logical_and(half, i == 7 - step))
        def _():
            w_first[0].wait_recv()
            w_next[1].start()

    ksib.wait_recv()

    def kchunk(buf, half, j):
        rows = aligned(j, 128)
        return jnp.concatenate([buf[half, 0, rows, :], buf[half, 1, rows, :]], axis=0)

    for b in range(4):

        def body(j, top):
            sc = nt(kchunk(kbuf, 0, j), qs[b])
            sbuf[b, aligned(j, CHUNK), :] = sc
            return jnp.maximum(top, fold8(sc, jnp.max))

        top = lax.fori_loop(0, b, body, jnp.full((8, GROUP), MASKED, F32))
        sc = nt(kchunk(kbuf, 0, b), qs[b])
        key_pos = lax.broadcasted_iota(jnp.int32, (CHUNK, GROUP), 0)
        row_pos = lax.rem(lax.broadcasted_iota(jnp.int32, (CHUNK, GROUP), 1), 128) + c * 128
        sc = jnp.where(key_pos <= row_pos, sc, MASKED)
        sbuf[b, b * CHUNK : (b + 1) * CHUNK, :] = sc
        stat[b] = jnp.maximum(top, fold8(sc, jnp.max))

    for copy in vc:
        copy.wait_recv()
    own_v.wait()
    vsib = rc(vbuf.at[0, c], vbuf.at[0, c], sib)
    go(vsib)

    @pl.when(lower)
    def _():
        for copy in kx:
            copy.wait_send()
        for copy in vx:
            copy.start()

    for d in range(4):
        uc[d].wait_recv()
    nc = [
        rc(
            n_ref.at[:, aligned(column_blocks[r] + ys[d], GROUP)],
            nbuf.at[r, my_rows],
            ydev(d),
        )
        for d in range(1, 4)
        for r in range(2)
    ]
    for copy in nc:
        go(copy)
    for b in range(4):
        for hd in range(4):
            cols = slice(hd * 128, hd * 128 + 128)
            ust[b, :, cols] = ubuf[b, :, cols].T
        kt[0, :, b * CHUNK : (b + 1) * CHUNK] = kchunk(kbuf, 0, b).T
    vsib.wait_recv()
    for b in range(4):
        vt[0, :, b * CHUNK : (b + 1) * CHUNK] = kchunk(vbuf, 0, b).T

    def across(buf):
        rows = [aligned(yfrom[d], 128) for d in range(4)]
        return [rc(buf.at[1, c, r], buf.at[1, c, r], sib) for r in rows]

    kxs = across(kbuf)
    vxs = rc(vbuf.at[1, c], vbuf.at[1, c], sib)

    @pl.when(upper)
    def _():
        for d in range(4):
            kx[d].wait_recv()
            kxs[d].start()
            kxs[d].wait_recv()
            part = kchunk(kbuf, 1, yfrom[d])
            kt[1, :, aligned(yfrom[d], CHUNK)] = part.T

            def body(b, carry):
                sc = nt(part, qs[b])
                sbuf[b, aligned(yfrom[d] + 4, CHUNK), :] = sc
                stat[b] = jnp.maximum(stat[b], fold8(sc, jnp.max))
                return carry

            lax.fori_loop(0, 4, body, 0)

    for b in range(4):
        shift = jnp.max(stat[b], axis=0, keepdims=True) * (FACTOR * LOG2E)

        def body(j, total):
            e = jnp.exp2(sbuf[b, aligned(j, CHUNK), :] * (FACTOR * LOG2E) - shift)
            ebuf[b, aligned(j, CHUNK), :] = e.astype(BF16)
            return total + fold8(e, jnp.sum)

        total = lax.fori_loop(0, b + 1, body, jnp.zeros((8, GROUP), F32))
        total = lax.fori_loop(4, 4 + 4 * h, body, total)
        inverse = 1.0 / jnp.sum(total, axis=0, keepdims=True)
        stat[b] = jnp.broadcast_to(inverse, (8, GROUP))
        ust[b] = (ust[b].astype(F32) * inverse).astype(BF16)

    def split(term, own, send, rows):
        first, second = term[:128], term[128:]
        own[rows, :] = jnp.where(c == 0, first, second)
        send[rows, :] = jnp.where(c == 0, second, first).astype(BF16)

    def remote_terms(product, right, own, send):
        def body(j, carry):
            term = product(ebuf[0, aligned(j + 4, CHUNK), :], right[0])
            for b in range(1, 4):
                term += product(ebuf[b, aligned(j + 4, CHUNK), :], right[b])
            split(term, own, send, aligned(j, 128))
            return carry

        lax.fori_loop(0, 4, body, 0)

    def own_terms(product, right, own, send):
        for j in range(4):
            term = product(ebuf[j, j * CHUNK : (j + 1) * CHUNK, :], right[j])
            for b in range(j + 1, 4):
                term += product(ebuf[b, j * CHUNK : (j + 1) * CHUNK, :], right[b])
            split(term, own, send, slice(j * 128, j * 128 + 128))

    dvxs = rc(dvsend.at[1], dvsib.at[1], sib)
    dvos = rc(dvsend.at[0], dvsib.at[0], sib)
    forward_w(lower, 0)
    block_rows = [slice(b * 128, b * 128 + 128) for b in range(4)]
    dvx = [rc(dvcs.at[r], dvcr.at[r], zdev(8)) for r in block_rows]

    @pl.when(upper)
    def _():
        remote_terms(nt, ust, dvown.at[1], dvsend.at[1])
        dvxs.start()

    own_terms(nt, ust, dvown.at[0], dvsend.at[0])
    go(dvos)
    forward_w(lower, 1)

    @pl.when(upper)
    def _():
        dvxs.wait_recv()
        dvcs[...] = (dvown[1] + dvsib[1].astype(F32)).astype(BF16)
        for copy in dvx:
            copy.start()

    my_head = aligned(y, 128)
    dvb = [
        [rc(dvfull.at[r, my_head], dvfull.at[r, my_head], ydev(d)) for d in range(1, 4)]
        for r in block_rows
    ]

    dvos.wait_recv()

    @pl.when(upper)
    def _():
        dvfull[:, my_head] = (dvown[0] + dvsib[0].astype(F32)).astype(BF16)
        for copies in dvb:
            for copy in copies:
                copy.start()
        for d in range(4):
            vx[d].wait_recv()
        vxs.start()
        vxs.wait_recv()
        for j in range(4):
            vt[1, :, j * CHUNK : (j + 1) * CHUNK] = kchunk(vbuf, 1, j).T

    forward_w(upper, 0)

    def by_keys(t, b):
        def far(_, total):
            return total + nn(t[1], ebuf[b, 1024:2048, :])

        near = nn(t[0, :, : (b + 1) * CHUNK], ebuf[b, : (b + 1) * CHUNK, :])
        return lax.fori_loop(0, h, far, near)

    for b in range(4):
        out = by_keys(vt, b)
        delta = jnp.sum(ust[b].astype(F32) * out, axis=0, keepdims=True) * stat[b, 0:1, :]

        def grads(j, carry):
            dp = nn(kchunk(vbuf, j // 4, lax.rem(j, 4)), ust[b])
            e = ebuf[b, aligned(j, CHUNK), :].astype(F32)
            ebuf[b, aligned(j, CHUNK), :] = (e * (dp - delta)).astype(BF16)
            return carry

        lax.fori_loop(0, b + 1, grads, 0)
        lax.fori_loop(4, 4 + 4 * h, grads, 0)

    dkxs = rc(dksend.at[1], dksib.at[1], sib)
    dkos = rc(dksend.at[0], dksib.at[0], sib)
    dkx = rc(dkcs, dkcr, zdev(8))

    @pl.when(upper)
    def _():
        remote_terms(nn, qs, dkown.at[1], dksend.at[1])
        dkxs.start()

    own_terms(nn, qs, dkown.at[0], dksend.at[0])
    go(dkos)

    forward_w(lower, 2)
    forward_w(upper, 1)

    def weight_grad():
        for copy in nc:
            copy.wait_recv()
        for copy in own_n:
            copy.wait()
        for copies in dvb:
            for copy in copies:
                copy.wait_recv()
        for r in (1, 0):
            rsend[r] = tn(nbuf[r, :, aligned(1 - c, CHUNK)], dvfull[...]).astype(BF16)
            rs[r].start()
        for r in (1, 0):
            rown = tn(nbuf[r, :, aligned(c, CHUNK)], dvfull[...])
            rs[r].wait_recv()
            total = (rown + rsib[r].astype(F32)).astype(BF16)
            for p in range(8):
                row = pl.multiple_of(column_blocks[r] * 16 + p // 4 * 32, 32)
                rfull[p % 4, pl.ds(row, 32), :] = total[p * 32 : p * 32 + 32]
            for copy in z1[r]:
                copy.start()

    rs = [rc(rsend.at[r], rsib.at[r], sib) for r in range(2)]
    za, zb = z // 4, lax.rem(z, 4)

    def group_dev(d):
        t = za * 4 + lax.rem(zb + d, 4)
        return {"dp": lax.rem(t, 8)}

    z_rows = [pl.ds(pl.multiple_of(column_blocks[r] * 16, 64), 64) for r in range(2)]
    z1 = [
        [
            rc(
                rfull.at[lax.rem(zb + d, 4), z_rows[r]],
                z1recv.at[d - 1, z_rows[r]],
                group_dev(d),
            )
            for d in range(1, 4)
        ]
        for r in range(2)
    ]

    for b in range(4):
        total = by_keys(kt, b)
        total = total * FACTOR
        for hd in range(4):
            cols = slice(hd * 128, hd * 128 + 128)
            dqs[b, :, cols] = total[:, cols].T.astype(BF16)
    dqc = [rc(dqs.at[ys[d]], dq_o.at[:, my_group], ydev(d)) for d in range(1, 4)]
    for copy in dqc:
        go(copy)
    out_dq = lc(dqs.at[y], dq_o.at[:, my_group])
    out_dq.start()

    @pl.when(upper)
    def _():
        for copy in dvx:
            copy.wait_send()
        dkxs.wait_recv()
        dkcs[...] = ((dkown[1] + dksib[1].astype(F32)) * FACTOR).astype(BF16)
        dkx.start()

    @pl.when(upper)
    def _():
        weight_grad()

    dkos.wait_recv()
    dkc = [
        rc(dkfin.at[aligned(ys[d], 128)], dk_o.at[:, my_head], ydev(d)) for d in range(1, 4)
    ]

    out_dk = lc(dkfin.at[my_rows], dk_o.at[:, my_head])

    def send_dk():
        for copy in dkc:
            copy.start()
        out_dk.start()

    @pl.when(upper)
    def _():
        dkfin[...] = ((dkown[0] + dksib[0].astype(F32)) * FACTOR).astype(BF16)
        send_dk()

    @pl.when(lower)
    def _():
        start_w()
        for b in range(4):
            dvx[b].wait_recv()
            r = block_rows[b]
            dvfull[r, my_head] = (
                dvown[0, r, :] + dvsib[0, r, :].astype(F32) + dvcr[r, :].astype(F32)
            ).astype(BF16)
            for copy in dvb[b]:
                copy.start()
        weight_grad()

    forward_w(upper, 2)
    @pl.when(jnp.logical_or(i == 3, i == 4))
    def _():
        w_first[0].wait_recv()

    ws2 = rc(wbuf.at[1, c], wbuf.at[1, c], sib)
    go(ws2)
    def z2copy(target, slot):
        dev = {"dp": target % 2 * 4 + zb, "seq": target // 2 * 8 + y * 2 + c}
        return rc(tfull.at[aligned(target, 32)], z2recv.at[slot], dev)

    other = [(1 - h) * 2 + lax.rem(za + e, 2) for e in range(2)]
    near = za + 1 - 2 * lax.rem(za, 2)
    z2 = [[z2copy(near, 0)], [z2copy(other[0], 1), z2copy(other[1], 2)]]
    for r in (1, 0):
        for copy in z1[r]:
            copy.wait_recv()
        total = rfull[zb, z_rows[r], :].astype(F32)
        for d in range(3):
            total += z1recv[d, z_rows[r], :].astype(F32)
        tfull[z_rows[r], :] = total.astype(BF16)
        for copy in z2[r]:
            go(copy)

    wsib.wait_recv()
    own_w.wait()
    ws2.wait_recv()
    for r in range(2):
        for cc in range(2):
            gns[r, :, cc * CHUNK : (cc + 1) * CHUNK] = nt(dvfull[...], wbuf[r, cc]).astype(BF16)
    gc = []
    out_gn = []
    for r in range(2):
        cols = aligned(column_blocks[r] + y, GROUP)
        for d in range(1, 4):
            copy = rc(gns.at[r, aligned(ys[d], 128)], gn_o.at[:, cols], ydev(d))
            gc.append(copy)
            go(copy)
        out_gn.append(lc(gns.at[r, my_rows], gn_o.at[:, cols]))
        out_gn[r].start()

    @pl.when(lower)
    def _():
        dkx.wait_recv()
        dkfin[...] = (
            (dkown[0] + dksib[0].astype(F32)) * FACTOR + dkcr[...].astype(F32)
        ).astype(BF16)
        send_dk()

    my_piece = aligned(i, 32)
    total = tfull[aligned(za, 32), :].astype(F32)
    for copy in z2[0] + z2[1]:
        copy.wait_recv()
    for d in range(3):
        total += z2recv[d].astype(F32)
    zfin[my_piece, :] = total.astype(BF16)
    far_piece = aligned(lax.rem(i + 4, 8), 32)
    p1 = rc(zfin.at[my_piece], zfin.at[my_piece], {"dp": lax.rem(i + 4, 8)})
    go(p1)
    pc = [rc(zfin.at[my_piece], dw_o.at[my_piece], group_dev(d)) for d in range(1, 4)]
    for copy in pc:
        go(copy)
    p1.wait_recv()
    pf = [rc(zfin.at[far_piece], dw_o.at[far_piece], group_dev(d)) for d in range(1, 4)]
    for copy in pf:
        go(copy)
    out_dw = [lc(zfin.at[p], dw_o.at[p]) for p in (my_piece, far_piece)]
    for copy in out_dw:
        copy.start()
    for copy in pc + pf:
        copy.wait_recv()

    for copy in [out_dq, out_dk] + out_dw + out_gn:
        copy.wait()
    for copy in dqc + dkc + gc:
        copy.wait_recv()
    for copy in started + dkc + rs + [copy for copies in dvb + z1 for copy in copies]:
        copy.wait_send()

    @pl.when(lower)
    def _():
        for copy in vx:
            copy.wait_send()

    @pl.when(upper)
    def _():
        for copy in kxs + [vxs, dvxs, dkxs, dkx]:
            copy.wait_send()

    @pl.when(jnp.logical_or(first_up, first_down))
    def _():
        w_first[0].wait_send()

    @pl.when(jnp.logical_and(i != 3, i != 4))
    def _():
        w_next[0].wait_send()


def local(queries, keys, values, grad_next, normed, value_weight):
    anywhere = pl.BlockSpec(memory_space=pl.ANY)

    def buf(*shape, dtype=BF16):
        return pltpu.VMEM(shape, dtype)

    count = 100
    dq, dk, gn, dw = pl.pallas_call(
        kernel,
        out_shape=(
            jax.ShapeDtypeStruct((128, 2048), BF16),
            jax.ShapeDtypeStruct((128, 512), BF16),
            jax.ShapeDtypeStruct((128, 4096), BF16),
            jax.ShapeDtypeStruct((256, 512), BF16),
        ),
        in_specs=[anywhere] * 6,
        out_specs=(anywhere,) * 4,
        scratch_shapes=[
            buf(2, 2, 512, 128),
            buf(2, 2, 512, 128),
            buf(4, 128, GROUP),
            buf(4, 128, GROUP),
            buf(2, 512, GROUP),
            buf(2, 2, 256, 512),
            buf(4, 2048, GROUP, dtype=F32),
            buf(4, 2048, GROUP),
            buf(4, GROUP, HEAD),
            buf(4, HEAD, GROUP),
            buf(2, HEAD, 1024),
            buf(2, HEAD, 1024),
            buf(4, 8, GROUP, dtype=F32),
            buf(2, 512, 128),
            buf(2, 512, 128, dtype=F32),
            buf(2, 512, 128),
            buf(512, 128),
            buf(512, 128),
            buf(2, 512, 128),
            buf(2, 512, 128, dtype=F32),
            buf(2, 512, 128),
            buf(512, 128),
            buf(512, 128),
            buf(512, 512),
            buf(512, 128),
            buf(4, 128, GROUP),
            buf(2, 256, 512),
            buf(2, 256, 512),
            buf(4, 128, 512),
            buf(3, 128, 512),
            buf(128, 512),
            buf(3, 32, 512),
            buf(256, 512),
            buf(2, 512, GROUP),
            pltpu.SemaphoreType.DMA((count,)),
            pltpu.SemaphoreType.DMA((count,)),
            pltpu.SemaphoreType.DMA((16,)),
        ],
        compiler_params=pltpu.CompilerParams(
            collective_id=0, has_side_effects=True, vmem_limit_bytes=60 * 1024 * 1024
        ),
        cost_estimate=pl.CostEstimate(
            flops=6_000_000_000, bytes_accessed=5_000_000, transcendentals=3_000_000
        ),
    )(queries[0, 0], keys[0, 0], values[0, 0], grad_next[0, 0], normed[0, 0], value_weight[0])
    return dq[None, None], dk[None, None], gn[None, None], dw.astype(F32)[None]


def solution(mesh):
    placed = (
        P("pipe", "dp", "seq", None),
        P("pipe", "dp", "seq", None),
        P("pipe", "dp", "seq", None),
        P("pipe", "dp", "seq", None),
        P("pipe", "dp", "seq", None),
        P("pipe", "seq", None),
    )
    return jax.shard_map(
        local,
        mesh=mesh,
        in_specs=placed,
        out_specs=(
            P("pipe", "dp", "seq", None),
            P("pipe", "dp", "seq", None),
            P("pipe", "dp", "seq", None),
            P("pipe", "seq", None),
        ),
        check_vma=False,
    )
```

```python
import functools

import jax
import jax.numpy as jnp
from jax import lax
from jax.experimental import pallas as pl
from jax.experimental.pallas import tpu as pltpu
from jax.sharding import PartitionSpec as P

HEAD = 128
HQ = 16
CHUNK = 256
GROUP = 512
FACTOR = HEAD**-0.5
LOG2E = 1.4426950408889634
MASKED = -1e30
MESH = pl.DeviceIdType.MESH
F32 = jnp.float32
BF16 = jnp.bfloat16


def nt(a, b):
    return lax.dot_general(a, b, (((1,), (1,)), ((), ())), preferred_element_type=F32)


def nn(a, b):
    return lax.dot_general(a, b, (((1,), (0,)), ((), ())), preferred_element_type=F32)


def tn(a, b):
    return lax.dot_general(a, b, (((0,), (0,)), ((), ())), preferred_element_type=F32)


def aligned(index, size):
    return pl.ds(pl.multiple_of(index * size, size), size)


def fold8(x, op):
    return op(x.reshape(CHUNK // 8, 8, GROUP), axis=0)


def kernel(
    q_ref,
    k_ref,
    v_ref,
    g_ref,
    n_ref,
    w_ref,
    dq_o,
    dk_o,
    gn_o,
    dw_o,
    kbuf,
    vbuf,
    qbuf,
    ubuf,
    nbuf,
    wbuf,
    sbuf,
    ebuf,
    qs,
    ust,
    kt,
    vt,
    stat,
    dvsend,
    dvown,
    dvsib,
    dvcs,
    dvcr,
    dksend,
    dkown,
    dksib,
    dkcs,
    dkcr,
    dvfull,
    dkfin,
    dqs,
    rsend,
    rsib,
    rfull,
    z1recv,
    tfull,
    z2recv,
    zfin,
    gns,
    send_sems,
    recv_sems,
    local_sems,
):
    i = lax.axis_index("dp")
    x = lax.axis_index("pipe")
    s = lax.axis_index("seq")
    h = s // 8
    y = lax.rem(s // 2, 4)
    c = lax.rem(s, 2)
    z = h * 8 + i
    lower = h == 0
    upper = h == 1
    used = [0]
    local_used = [0]
    started = []

    def lc(src, dst):
        n = local_used[0]
        local_used[0] += 1
        return pltpu.make_async_copy(src, dst, local_sems.at[n])

    def rc(src, dst, dev):
        n = used[0]
        used[0] += 1
        return pltpu.make_async_remote_copy(
            src_ref=src,
            dst_ref=dst,
            send_sem=send_sems.at[n],
            recv_sem=recv_sems.at[n],
            device_id=dev,
            device_id_type=MESH,
        )

    def go(copy):
        copy.start()
        started.append(copy)

    def ydev(d):
        return {"seq": h * 8 + lax.rem(y + d, 4) * 2 + c}

    def zdev(d):
        t = lax.rem(z + d, 16)
        return {"dp": lax.rem(t, 8), "seq": (t // 8) * 8 + y * 2 + c}

    sib = {"seq": s + 1 - 2 * c}
    ys = [lax.rem(y + d, 4) for d in range(4)]
    yfrom = [lax.rem(y + 4 - d, 4) for d in range(4)]

    bar = pltpu.get_barrier_semaphore()
    count = 0
    for d in range(1, 4):
        pl.semaphore_signal(bar, inc=1, device_id=ydev(d), device_id_type=MESH)
        count += 1
    for d in range(4):
        pl.semaphore_signal(
            bar,
            inc=1,
            device_id={"pipe": lax.rem(x + 1, 4), "seq": ydev(d)["seq"]},
            device_id_type=MESH,
        )
        count += 1
    pl.semaphore_signal(bar, inc=1, device_id=sib, device_id_type=MESH)
    count += 1
    for d in range(1, 8):
        dev = {"dp": lax.rem(i + d, 8)}
        pl.semaphore_signal(bar, inc=1, device_id=dev, device_id_type=MESH)
        count += 1
    for d in (1, 4, 8, 12, 15):
        pl.semaphore_signal(bar, inc=1, device_id=zdev(d), device_id_type=MESH)
        count += 1
    my_rows = aligned(y, 128)
    my_group = aligned(y, GROUP)
    column_blocks = [lax.rem(h + r, 2) * 4 for r in range(2)]
    own_k = lc(k_ref.at[:, my_rows], kbuf.at[0, c, my_rows])
    own_q = lc(q_ref.at[:, my_group], qbuf.at[y])
    own_v = lc(v_ref.at[:, my_rows], vbuf.at[0, c, my_rows])
    own_w = lc(w_ref, wbuf.at[0, c])
    own_n = [
        lc(n_ref.at[:, aligned(column_blocks[r] + y, GROUP)], nbuf.at[r, my_rows])
        for r in range(2)
    ]
    for copy in [own_k, own_q, own_v, own_w] + own_n:
        copy.start()
    pl.semaphore_wait(bar, count)

    kc = [
        rc(k_ref.at[:, aligned(ys[d], 128)], kbuf.at[0, c, my_rows], ydev(d)) for d in range(1, 4)
    ]
    for copy in kc:
        go(copy)

    def crossing(ref, buf):
        copies = []
        for d in range(4):
            rows = aligned(yfrom[d], 128)
            src = ref.at[:, my_rows] if d == 0 else buf.at[0, c, rows]
            copies.append(rc(src, buf.at[1, c, rows], zdev(8)))
        return copies

    kx = crossing(k_ref, kbuf)

    @pl.when(lower)
    def _():
        kx[0].start()

    qc = [
        rc(q_ref.at[:, aligned(ys[d], GROUP)], qbuf.at[y], ydev(d)) for d in range(1, 4)
    ]
    for copy in qc:
        go(copy)
    vx = crossing(v_ref, vbuf)
    uc = [
        rc(
            g_ref.at[:, aligned(ys[d], GROUP)],
            ubuf.at[y],
            {"pipe": lax.rem(x + 3, 4), "seq": ydev(d)["seq"]},
        )
        for d in range(4)
    ]
    for copy in uc:
        go(copy)

    for d in range(1, 4):
        kc[d - 1].wait_recv()

        @pl.when(lower)
        def _():
            kx[d].start()

    own_k.wait()
    ksib = rc(kbuf.at[0, c], kbuf.at[0, c], sib)
    go(ksib)
    for d in range(1, 4):
        qc[d - 1].wait_recv()
    own_q.wait()
    vc = [
        rc(v_ref.at[:, aligned(ys[d], 128)], vbuf.at[0, c, my_rows], ydev(d)) for d in range(1, 4)
    ]
    for copy in vc:
        go(copy)
    for b in range(4):
        for hd in range(4):
            qs[b, hd * 128 : hd * 128 + 128, :] = qbuf[b, :, hd * 128 : hd * 128 + 128]


    wsib = rc(w_ref, wbuf.at[0, c], sib)
    go(wsib)
    n = used[0]
    used[0] += 2

    def wcopy(src, which, d):
        return pltpu.make_async_remote_copy(
            src_ref=src,
            dst_ref=wbuf.at[1, c],
            send_sem=send_sems.at[n + which],
            recv_sem=recv_sems.at[n],
            device_id=zdev(d),
            device_id_type=MESH,
        )

    first_up = i == 7
    first_down = i == 0

    def start_w():
        @pl.when(first_down)
        def _():
            w_first[0].start()

        @pl.when(first_up)
        def _():
            w_first[1].start()

    w_first = [wcopy(w_ref, 0, 15), wcopy(w_ref, 0, 1)]
    w_next = [wcopy(wbuf.at[1, c], 1, 1), wcopy(wbuf.at[1, c], 1, 15)]

    @pl.when(upper)
    def _():
        start_w()

    def forward_w(half, step):
        @pl.when(jnp.logical_and(half, i == step))
        def _():
            w_first[0].wait_recv()
            w_next[0].start()

        @pl.when(jnp.logical_and(half, i == 7 - step))
        def _():
            w_first[0].wait_recv()
            w_next[1].start()

    ksib.wait_recv()

    def kchunk(buf, half, j):
        rows = aligned(j, 128)
        return jnp.concatenate([buf[half, 0, rows, :], buf[half, 1, rows, :]], axis=0)

    for b in range(4):

        def body(j, top):
            sc = nt(kchunk(kbuf, 0, j), qs[b])
            sbuf[b, aligned(j, CHUNK), :] = sc
            return jnp.maximum(top, fold8(sc, jnp.max))

        top = lax.fori_loop(0, b, body, jnp.full((8, GROUP), MASKED, F32))
        sc = nt(kchunk(kbuf, 0, b), qs[b])
        key_pos = lax.broadcasted_iota(jnp.int32, (CHUNK, GROUP), 0)
        row_pos = lax.rem(lax.broadcasted_iota(jnp.int32, (CHUNK, GROUP), 1), 128) + c * 128
        sc = jnp.where(key_pos <= row_pos, sc, MASKED)
        sbuf[b, b * CHUNK : (b + 1) * CHUNK, :] = sc
        stat[b] = jnp.maximum(top, fold8(sc, jnp.max))

    for copy in vc:
        copy.wait_recv()
    own_v.wait()
    vsib = rc(vbuf.at[0, c], vbuf.at[0, c], sib)
    go(vsib)

    @pl.when(lower)
    def _():
        for copy in kx:
            copy.wait_send()
        for copy in vx:
            copy.start()

    for b in range(4):
        kt[0, :, b * CHUNK : (b + 1) * CHUNK] = kchunk(kbuf, 0, b).T

    def across(buf):
        rows = [aligned(yfrom[d], 128) for d in range(4)]
        return [rc(buf.at[1, c, r], buf.at[1, c, r], sib) for r in rows]

    kxs = across(kbuf)
    vxs = rc(vbuf.at[1, c], vbuf.at[1, c], sib)

    @pl.when(upper)
    def _():
        for d in range(4):
            kx[d].wait_recv()
            kxs[d].start()
            kxs[d].wait_recv()
            part = kchunk(kbuf, 1, yfrom[d])
            kt[1, :, aligned(yfrom[d], CHUNK)] = part.T

            def body(b, carry):
                sc = nt(part, qs[b])
                sbuf[b, aligned(yfrom[d] + 4, CHUNK), :] = sc
                stat[b] = jnp.maximum(stat[b], fold8(sc, jnp.max))
                return carry

            lax.fori_loop(0, 4, body, 0)

    for d in range(4):
        uc[d].wait_recv()
    nc = [
        rc(
            n_ref.at[:, aligned(column_blocks[r] + ys[d], GROUP)],
            nbuf.at[r, my_rows],
            ydev(d),
        )
        for d in range(1, 4)
        for r in range(2)
    ]
    for copy in nc:
        go(copy)
    for b in range(4):
        for hd in range(4):
            cols = slice(hd * 128, hd * 128 + 128)
            ust[b, :, cols] = ubuf[b, :, cols].T

    for b in range(4):
        shift = jnp.max(stat[b], axis=0, keepdims=True) * (FACTOR * LOG2E)

        def body(j, total):
            e = jnp.exp2(sbuf[b, aligned(j, CHUNK), :] * (FACTOR * LOG2E) - shift)
            ebuf[b, aligned(j, CHUNK), :] = e.astype(BF16)
            return total + fold8(e, jnp.sum)

        total = lax.fori_loop(0, b + 1, body, jnp.zeros((8, GROUP), F32))
        total = lax.fori_loop(4, 4 + 4 * h, body, total)
        inverse = 1.0 / jnp.sum(total, axis=0, keepdims=True)
        stat[b] = jnp.broadcast_to(inverse, (8, GROUP))
        ust[b] = (ust[b].astype(F32) * inverse).astype(BF16)

    def split(term, own, send, rows):
        first, second = term[:128], term[128:]
        own[rows, :] = jnp.where(c == 0, first, second)
        send[rows, :] = jnp.where(c == 0, second, first).astype(BF16)

    def remote_terms(product, right, own, send):
        def body(j, carry):
            term = product(ebuf[0, aligned(j + 4, CHUNK), :], right[0])
            for b in range(1, 4):
                term += product(ebuf[b, aligned(j + 4, CHUNK), :], right[b])
            split(term, own, send, aligned(j, 128))
            return carry

        lax.fori_loop(0, 4, body, 0)

    def own_terms(product, right, own, send):
        for j in range(4):
            term = product(ebuf[j, j * CHUNK : (j + 1) * CHUNK, :], right[j])
            for b in range(j + 1, 4):
                term += product(ebuf[b, j * CHUNK : (j + 1) * CHUNK, :], right[b])
            split(term, own, send, slice(j * 128, j * 128 + 128))

    dvxs = rc(dvsend.at[1], dvsib.at[1], sib)
    dvos = rc(dvsend.at[0], dvsib.at[0], sib)
    forward_w(lower, 0)
    block_rows = [slice(b * 128, b * 128 + 128) for b in range(4)]
    dvx = [rc(dvcs.at[r], dvcr.at[r], zdev(8)) for r in block_rows]

    @pl.when(upper)
    def _():
        remote_terms(nt, ust, dvown.at[1], dvsend.at[1])
        dvxs.start()

    own_terms(nt, ust, dvown.at[0], dvsend.at[0])
    go(dvos)
    forward_w(lower, 1)

    @pl.when(upper)
    def _():
        dvxs.wait_recv()
        dvcs[...] = (dvown[1] + dvsib[1].astype(F32)).astype(BF16)
        for copy in dvx:
            copy.start()

    my_head = aligned(y, 128)
    dvb = [
        [rc(dvfull.at[r, my_head], dvfull.at[r, my_head], ydev(d)) for d in range(1, 4)]
        for r in block_rows
    ]

    dvos.wait_recv()

    @pl.when(upper)
    def _():
        dvfull[:, my_head] = (dvown[0] + dvsib[0].astype(F32)).astype(BF16)
        for copies in dvb:
            for copy in copies:
                copy.start()
        for d in range(4):
            vx[d].wait_recv()
        vxs.start()
        vxs.wait_recv()
        for j in range(4):
            vt[1, :, j * CHUNK : (j + 1) * CHUNK] = kchunk(vbuf, 1, j).T

    forward_w(upper, 0)

    vsib.wait_recv()
    for b in range(4):
        vt[0, :, b * CHUNK : (b + 1) * CHUNK] = kchunk(vbuf, 0, b).T

    def by_keys(t, b):
        def far(_, total):
            return total + nn(t[1], ebuf[b, 1024:2048, :])

        near = nn(t[0, :, : (b + 1) * CHUNK], ebuf[b, : (b + 1) * CHUNK, :])
        return lax.fori_loop(0, h, far, near)

    for b in range(4):
        out = by_keys(vt, b)
        delta = jnp.sum(ust[b].astype(F32) * out, axis=0, keepdims=True) * stat[b, 0:1, :]

        def grads(j, carry):
            dp = nn(kchunk(vbuf, j // 4, lax.rem(j, 4)), ust[b])
            e = ebuf[b, aligned(j, CHUNK), :].astype(F32)
            ebuf[b, aligned(j, CHUNK), :] = (e * (dp - delta)).astype(BF16)
            return carry

        lax.fori_loop(0, b + 1, grads, 0)
        lax.fori_loop(4, 4 + 4 * h, grads, 0)

    dkxs = rc(dksend.at[1], dksib.at[1], sib)
    dkos = rc(dksend.at[0], dksib.at[0], sib)
    dkx = rc(dkcs, dkcr, zdev(8))

    @pl.when(upper)
    def _():
        remote_terms(nn, qs, dkown.at[1], dksend.at[1])
        dkxs.start()

    own_terms(nn, qs, dkown.at[0], dksend.at[0])
    go(dkos)

    forward_w(lower, 2)
    forward_w(upper, 1)

    def weight_grad():
        for copy in nc:
            copy.wait_recv()
        for copy in own_n:
            copy.wait()
        for copies in dvb:
            for copy in copies:
                copy.wait_recv()
        for r in (1, 0):
            rsend[r] = tn(nbuf[r, :, aligned(1 - c, CHUNK)], dvfull[...]).astype(BF16)
            rs[r].start()
        for r in (1, 0):
            rown = tn(nbuf[r, :, aligned(c, CHUNK)], dvfull[...])
            rs[r].wait_recv()
            total = (rown + rsib[r].astype(F32)).astype(BF16)
            for p in range(8):
                row = pl.multiple_of(column_blocks[r] * 16 + p // 4 * 32, 32)
                rfull[p % 4, pl.ds(row, 32), :] = total[p * 32 : p * 32 + 32]
            for copy in z1[r]:
                copy.start()

    rs = [rc(rsend.at[r], rsib.at[r], sib) for r in range(2)]
    za, zb = z // 4, lax.rem(z, 4)

    def group_dev(d):
        t = za * 4 + lax.rem(zb + d, 4)
        return {"dp": lax.rem(t, 8)}

    z_rows = [pl.ds(pl.multiple_of(column_blocks[r] * 16, 64), 64) for r in range(2)]
    z1 = [
        [
            rc(
                rfull.at[lax.rem(zb + d, 4), z_rows[r]],
                z1recv.at[d - 1, z_rows[r]],
                group_dev(d),
            )
            for d in range(1, 4)
        ]
        for r in range(2)
    ]

    for b in range(4):
        total = by_keys(kt, b)
        total = total * FACTOR
        for hd in range(4):
            cols = slice(hd * 128, hd * 128 + 128)
            dqs[b, :, cols] = total[:, cols].T.astype(BF16)
    dqc = [rc(dqs.at[ys[d]], dq_o.at[:, my_group], ydev(d)) for d in range(1, 4)]
    for copy in dqc:
        go(copy)
    out_dq = lc(dqs.at[y], dq_o.at[:, my_group])
    out_dq.start()

    @pl.when(upper)
    def _():
        for copy in dvx:
            copy.wait_send()
        dkxs.wait_recv()
        dkcs[...] = ((dkown[1] + dksib[1].astype(F32)) * FACTOR).astype(BF16)
        dkx.start()

    @pl.when(upper)
    def _():
        weight_grad()

    dkos.wait_recv()
    dkc = [
        rc(dkfin.at[aligned(ys[d], 128)], dk_o.at[:, my_head], ydev(d)) for d in range(1, 4)
    ]

    out_dk = lc(dkfin.at[my_rows], dk_o.at[:, my_head])

    def send_dk():
        for copy in dkc:
            copy.start()
        out_dk.start()

    @pl.when(upper)
    def _():
        dkfin[...] = ((dkown[0] + dksib[0].astype(F32)) * FACTOR).astype(BF16)
        send_dk()

    @pl.when(lower)
    def _():
        start_w()
        for b in range(4):
            dvx[b].wait_recv()
            r = block_rows[b]
            dvfull[r, my_head] = (
                dvown[0, r, :] + dvsib[0, r, :].astype(F32) + dvcr[r, :].astype(F32)
            ).astype(BF16)
            for copy in dvb[b]:
                copy.start()
        weight_grad()

    forward_w(upper, 2)
    @pl.when(jnp.logical_or(i == 3, i == 4))
    def _():
        w_first[0].wait_recv()

    ws2 = rc(wbuf.at[1, c], wbuf.at[1, c], sib)
    go(ws2)
    def z2copy(target, slot):
        dev = {"dp": target % 2 * 4 + zb, "seq": target // 2 * 8 + y * 2 + c}
        return rc(tfull.at[aligned(target, 32)], z2recv.at[slot], dev)

    other = [(1 - h) * 2 + lax.rem(za + e, 2) for e in range(2)]
    near = za + 1 - 2 * lax.rem(za, 2)
    z2 = [[z2copy(near, 0)], [z2copy(other[0], 1), z2copy(other[1], 2)]]
    for r in (1, 0):
        for copy in z1[r]:
            copy.wait_recv()
        total = rfull[zb, z_rows[r], :].astype(F32)
        for d in range(3):
            total += z1recv[d, z_rows[r], :].astype(F32)
        tfull[z_rows[r], :] = total.astype(BF16)
        for copy in z2[r]:
            go(copy)

    wsib.wait_recv()
    own_w.wait()
    ws2.wait_recv()
    for r in range(2):
        for cc in range(2):
            gns[r, :, cc * CHUNK : (cc + 1) * CHUNK] = nt(dvfull[...], wbuf[r, cc]).astype(BF16)
    gc = []
    out_gn = []
    for r in range(2):
        cols = aligned(column_blocks[r] + y, GROUP)
        for d in range(1, 4):
            copy = rc(gns.at[r, aligned(ys[d], 128)], gn_o.at[:, cols], ydev(d))
            gc.append(copy)
            go(copy)
        out_gn.append(lc(gns.at[r, my_rows], gn_o.at[:, cols]))
        out_gn[r].start()

    my_piece = aligned(i, 32)
    total = tfull[aligned(za, 32), :].astype(F32)
    for copy in z2[0] + z2[1]:
        copy.wait_recv()
    for d in range(3):
        total += z2recv[d].astype(F32)
    zfin[my_piece, :] = total.astype(BF16)
    far_piece = aligned(lax.rem(i + 4, 8), 32)
    p1 = rc(zfin.at[my_piece], zfin.at[my_piece], {"dp": lax.rem(i + 4, 8)})
    go(p1)
    pc = [rc(zfin.at[my_piece], dw_o.at[my_piece], group_dev(d)) for d in range(1, 4)]
    for copy in pc:
        go(copy)
    p1.wait_recv()
    pf = [rc(zfin.at[far_piece], dw_o.at[far_piece], group_dev(d)) for d in range(1, 4)]
    for copy in pf:
        go(copy)
    out_dw = [lc(zfin.at[p], dw_o.at[p]) for p in (my_piece, far_piece)]
    for copy in out_dw:
        copy.start()
    @pl.when(lower)
    def _():
        dkx.wait_recv()
        dkfin[...] = (
            (dkown[0] + dksib[0].astype(F32)) * FACTOR + dkcr[...].astype(F32)
        ).astype(BF16)
        send_dk()

    for copy in pc + pf:
        copy.wait_recv()

    for copy in [out_dq, out_dk] + out_dw + out_gn:
        copy.wait()
    for copy in dqc + dkc + gc:
        copy.wait_recv()
    for copy in started + dkc + rs + [copy for copies in dvb + z1 for copy in copies]:
        copy.wait_send()

    @pl.when(lower)
    def _():
        for copy in vx:
            copy.wait_send()

    @pl.when(upper)
    def _():
        for copy in kxs + [vxs, dvxs, dkxs, dkx]:
            copy.wait_send()

    @pl.when(jnp.logical_or(first_up, first_down))
    def _():
        w_first[0].wait_send()

    @pl.when(jnp.logical_and(i != 3, i != 4))
    def _():
        w_next[0].wait_send()


def local(queries, keys, values, grad_next, normed, value_weight):
    anywhere = pl.BlockSpec(memory_space=pl.ANY)

    def buf(*shape, dtype=BF16):
        return pltpu.VMEM(shape, dtype)

    count = 100
    dq, dk, gn, dw = pl.pallas_call(
        kernel,
        out_shape=(
            jax.ShapeDtypeStruct((128, 2048), BF16),
            jax.ShapeDtypeStruct((128, 512), BF16),
            jax.ShapeDtypeStruct((128, 4096), BF16),
            jax.ShapeDtypeStruct((256, 512), BF16),
        ),
        in_specs=[anywhere] * 6,
        out_specs=(anywhere,) * 4,
        scratch_shapes=[
            buf(2, 2, 512, 128),
            buf(2, 2, 512, 128),
            buf(4, 128, GROUP),
            buf(4, 128, GROUP),
            buf(2, 512, GROUP),
            buf(2, 2, 256, 512),
            buf(4, 2048, GROUP, dtype=F32),
            buf(4, 2048, GROUP),
            buf(4, GROUP, HEAD),
            buf(4, HEAD, GROUP),
            buf(2, HEAD, 1024),
            buf(2, HEAD, 1024),
            buf(4, 8, GROUP, dtype=F32),
            buf(2, 512, 128),
            buf(2, 512, 128, dtype=F32),
            buf(2, 512, 128),
            buf(512, 128),
            buf(512, 128),
            buf(2, 512, 128),
            buf(2, 512, 128, dtype=F32),
            buf(2, 512, 128),
            buf(512, 128),
            buf(512, 128),
            buf(512, 512),
            buf(512, 128),
            buf(4, 128, GROUP),
            buf(2, 256, 512),
            buf(2, 256, 512),
            buf(4, 128, 512),
            buf(3, 128, 512),
            buf(128, 512),
            buf(3, 32, 512),
            buf(256, 512),
            buf(2, 512, GROUP),
            pltpu.SemaphoreType.DMA((count,)),
            pltpu.SemaphoreType.DMA((count,)),
            pltpu.SemaphoreType.DMA((16,)),
        ],
        compiler_params=pltpu.CompilerParams(
            collective_id=0, has_side_effects=True, vmem_limit_bytes=60 * 1024 * 1024
        ),
        cost_estimate=pl.CostEstimate(
            flops=6_000_000_000, bytes_accessed=5_000_000, transcendentals=3_000_000
        ),
    )(queries[0, 0], keys[0, 0], values[0, 0], grad_next[0, 0], normed[0, 0], value_weight[0])
    return dq[None, None], dk[None, None], gn[None, None], dw.astype(F32)[None]


def solution(mesh):
    placed = (
        P("pipe", "dp", "seq", None),
        P("pipe", "dp", "seq", None),
        P("pipe", "dp", "seq", None),
        P("pipe", "dp", "seq", None),
        P("pipe", "dp", "seq", None),
        P("pipe", "seq", None),
    )
    return jax.shard_map(
        local,
        mesh=mesh,
        in_specs=placed,
        out_specs=(
            P("pipe", "dp", "seq", None),
            P("pipe", "dp", "seq", None),
            P("pipe", "dp", "seq", None),
            P("pipe", "seq", None),
        ),
        check_vma=False,
    )
```

```python
import functools

import jax
import jax.numpy as jnp
from jax import lax
from jax.experimental import pallas as pl
from jax.experimental.pallas import tpu as pltpu
from jax.sharding import PartitionSpec as P

HEAD = 128
HQ = 16
CHUNK = 256
GROUP = 512
FACTOR = HEAD**-0.5
LOG2E = 1.4426950408889634
MASKED = -1e30
MESH = pl.DeviceIdType.MESH
F32 = jnp.float32
BF16 = jnp.bfloat16


def nt(a, b):
    return lax.dot_general(a, b, (((1,), (1,)), ((), ())), preferred_element_type=F32)


def nn(a, b):
    return lax.dot_general(a, b, (((1,), (0,)), ((), ())), preferred_element_type=F32)


def tn(a, b):
    return lax.dot_general(a, b, (((0,), (0,)), ((), ())), preferred_element_type=F32)


def aligned(index, size):
    return pl.ds(pl.multiple_of(index * size, size), size)


def fold8(x, op):
    return op(x.reshape(CHUNK // 8, 8, GROUP), axis=0)


def kernel(
    q_ref,
    k_ref,
    v_ref,
    g_ref,
    n_ref,
    w_ref,
    dq_o,
    dk_o,
    gn_o,
    dw_o,
    kbuf,
    vbuf,
    qbuf,
    ubuf,
    nbuf,
    wbuf,
    sbuf,
    ebuf,
    qs,
    ust,
    kt,
    vt,
    stat,
    dvsend,
    dvown,
    dvsib,
    dvcs,
    dvcr,
    dksend,
    dkown,
    dksib,
    dkcs,
    dkcr,
    dvfull,
    dkfin,
    dqs,
    rsend,
    rsib,
    rfull,
    z1recv,
    tfull,
    z2recv,
    zfin,
    gns,
    send_sems,
    recv_sems,
    local_sems,
):
    i = lax.axis_index("dp")
    x = lax.axis_index("pipe")
    s = lax.axis_index("seq")
    h = s // 8
    y = lax.rem(s // 2, 4)
    c = lax.rem(s, 2)
    z = h * 8 + i
    lower = h == 0
    upper = h == 1
    used = [0]
    local_used = [0]
    started = []

    def lc(src, dst):
        n = local_used[0]
        local_used[0] += 1
        return pltpu.make_async_copy(src, dst, local_sems.at[n])

    def rc(src, dst, dev):
        n = used[0]
        used[0] += 1
        return pltpu.make_async_remote_copy(
            src_ref=src,
            dst_ref=dst,
            send_sem=send_sems.at[n],
            recv_sem=recv_sems.at[n],
            device_id=dev,
            device_id_type=MESH,
        )

    def go(copy):
        copy.start()
        started.append(copy)

    def ydev(d):
        return {"seq": h * 8 + lax.rem(y + d, 4) * 2 + c}

    def zdev(d):
        t = lax.rem(z + d, 16)
        return {"dp": lax.rem(t, 8), "seq": (t // 8) * 8 + y * 2 + c}

    sib = {"seq": s + 1 - 2 * c}
    ys = [lax.rem(y + d, 4) for d in range(4)]
    yfrom = [lax.rem(y + 4 - d, 4) for d in range(4)]

    bar = pltpu.get_barrier_semaphore()
    count = 0
    for d in range(1, 4):
        pl.semaphore_signal(bar, inc=1, device_id=ydev(d), device_id_type=MESH)
        count += 1
    for d in range(4):
        pl.semaphore_signal(
            bar,
            inc=1,
            device_id={"pipe": lax.rem(x + 1, 4), "seq": ydev(d)["seq"]},
            device_id_type=MESH,
        )
        count += 1
    pl.semaphore_signal(bar, inc=1, device_id=sib, device_id_type=MESH)
    count += 1
    for d in range(1, 8):
        dev = {"dp": lax.rem(i + d, 8)}
        pl.semaphore_signal(bar, inc=1, device_id=dev, device_id_type=MESH)
        count += 1
    for d in (1, 4, 8, 12, 15):
        pl.semaphore_signal(bar, inc=1, device_id=zdev(d), device_id_type=MESH)
        count += 1
    my_rows = aligned(y, 128)
    my_group = aligned(y, GROUP)
    column_blocks = [lax.rem(h + r, 2) * 4 for r in range(2)]
    own_k = lc(k_ref.at[:, my_rows], kbuf.at[0, c, my_rows])
    own_q = lc(q_ref.at[:, my_group], qbuf.at[y])
    own_v = lc(v_ref.at[:, my_rows], vbuf.at[0, c, my_rows])
    own_w = lc(w_ref, wbuf.at[0, c])
    own_n = [
        lc(n_ref.at[:, aligned(column_blocks[r] + y, GROUP)], nbuf.at[r, my_rows])
        for r in range(2)
    ]
    for copy in [own_k, own_q, own_v, own_w] + own_n:
        copy.start()
    pl.semaphore_wait(bar, count)

    kc = [
        rc(k_ref.at[:, aligned(ys[d], 128)], kbuf.at[0, c, my_rows], ydev(d)) for d in range(1, 4)
    ]
    for copy in kc:
        go(copy)

    def crossing(ref, buf):
        copies = []
        for d in range(4):
            rows = aligned(yfrom[d], 128)
            src = ref.at[:, my_rows] if d == 0 else buf.at[0, c, rows]
            copies.append(rc(src, buf.at[1, c, rows], zdev(8)))
        return copies

    kx = crossing(k_ref, kbuf)

    @pl.when(lower)
    def _():
        kx[0].start()

    qc = [
        rc(q_ref.at[:, aligned(ys[d], GROUP)], qbuf.at[y], ydev(d)) for d in range(1, 4)
    ]
    vx = crossing(v_ref, vbuf)
    uc = [
        rc(
            g_ref.at[:, aligned(ys[d], GROUP)],
            ubuf.at[y],
            {"pipe": lax.rem(x + 3, 4), "seq": ydev(d)["seq"]},
        )
        for d in range(4)
    ]

    for d in range(1, 4):
        kc[d - 1].wait_recv()

        @pl.when(lower)
        def _():
            kx[d].start()

    own_k.wait()
    ksib = rc(kbuf.at[0, c], kbuf.at[0, c], sib)
    go(ksib)
    for copy in qc + uc:
        go(copy)
    for d in range(1, 4):
        qc[d - 1].wait_recv()
    own_q.wait()
    vc = [
        rc(v_ref.at[:, aligned(ys[d], 128)], vbuf.at[0, c, my_rows], ydev(d)) for d in range(1, 4)
    ]
    for copy in vc:
        go(copy)
    for b in range(4):
        for hd in range(4):
            qs[b, hd * 128 : hd * 128 + 128, :] = qbuf[b, :, hd * 128 : hd * 128 + 128]


    wsib = rc(w_ref, wbuf.at[0, c], sib)
    go(wsib)
    n = used[0]
    used[0] += 2

    def wcopy(src, which, d):
        return pltpu.make_async_remote_copy(
            src_ref=src,
            dst_ref=wbuf.at[1, c],
            send_sem=send_sems.at[n + which],
            recv_sem=recv_sems.at[n],
            device_id=zdev(d),
            device_id_type=MESH,
        )

    first_up = i == 7
    first_down = i == 0

    def start_w():
        @pl.when(first_down)
        def _():
            w_first[0].start()

        @pl.when(first_up)
        def _():
            w_first[1].start()

    w_first = [wcopy(w_ref, 0, 15), wcopy(w_ref, 0, 1)]
    w_next = [wcopy(wbuf.at[1, c], 1, 1), wcopy(wbuf.at[1, c], 1, 15)]

    @pl.when(upper)
    def _():
        start_w()

    def forward_w(half, step):
        @pl.when(jnp.logical_and(half, i == step))
        def _():
            w_first[0].wait_recv()
            w_next[0].start()

        @pl.when(jnp.logical_and(half, i == 7 - step))
        def _():
            w_first[0].wait_recv()
            w_next[1].start()

    ksib.wait_recv()

    def kchunk(buf, half, j):
        rows = aligned(j, 128)
        return jnp.concatenate([buf[half, 0, rows, :], buf[half, 1, rows, :]], axis=0)

    for b in range(4):

        def body(j, top):
            sc = nt(kchunk(kbuf, 0, j), qs[b])
            sbuf[b, aligned(j, CHUNK), :] = sc
            return jnp.maximum(top, fold8(sc, jnp.max))

        top = lax.fori_loop(0, b, body, jnp.full((8, GROUP), MASKED, F32))
        sc = nt(kchunk(kbuf, 0, b), qs[b])
        key_pos = lax.broadcasted_iota(jnp.int32, (CHUNK, GROUP), 0)
        row_pos = lax.rem(lax.broadcasted_iota(jnp.int32, (CHUNK, GROUP), 1), 128) + c * 128
        sc = jnp.where(key_pos <= row_pos, sc, MASKED)
        sbuf[b, b * CHUNK : (b + 1) * CHUNK, :] = sc
        stat[b] = jnp.maximum(top, fold8(sc, jnp.max))

    for copy in vc:
        copy.wait_recv()
    own_v.wait()
    vsib = rc(vbuf.at[0, c], vbuf.at[0, c], sib)
    go(vsib)

    @pl.when(lower)
    def _():
        for copy in kx:
            copy.wait_send()
        for copy in vx:
            copy.start()

    for b in range(4):
        kt[0, :, b * CHUNK : (b + 1) * CHUNK] = kchunk(kbuf, 0, b).T

    def across(buf):
        rows = [aligned(yfrom[d], 128) for d in range(4)]
        return [rc(buf.at[1, c, r], buf.at[1, c, r], sib) for r in rows]

    kxs = across(kbuf)
    vxs = rc(vbuf.at[1, c], vbuf.at[1, c], sib)

    @pl.when(upper)
    def _():
        for d in range(4):
            kx[d].wait_recv()
            kxs[d].start()
            kxs[d].wait_recv()
            part = kchunk(kbuf, 1, yfrom[d])
            kt[1, :, aligned(yfrom[d], CHUNK)] = part.T

            def body(b, carry):
                sc = nt(part, qs[b])
                sbuf[b, aligned(yfrom[d] + 4, CHUNK), :] = sc
                stat[b] = jnp.maximum(stat[b], fold8(sc, jnp.max))
                return carry

            lax.fori_loop(0, 4, body, 0)

    for d in range(4):
        uc[d].wait_recv()
    nc = [
        rc(
            n_ref.at[:, aligned(column_blocks[r] + ys[d], GROUP)],
            nbuf.at[r, my_rows],
            ydev(d),
        )
        for d in range(1, 4)
        for r in range(2)
    ]
    for copy in nc:
        go(copy)
    for b in range(4):
        for hd in range(4):
            cols = slice(hd * 128, hd * 128 + 128)
            ust[b, :, cols] = ubuf[b, :, cols].T

    for b in range(4):
        shift = jnp.max(stat[b], axis=0, keepdims=True) * (FACTOR * LOG2E)

        def body(j, total):
            e = jnp.exp2(sbuf[b, aligned(j, CHUNK), :] * (FACTOR * LOG2E) - shift)
            ebuf[b, aligned(j, CHUNK), :] = e.astype(BF16)
            return total + fold8(e, jnp.sum)

        total = lax.fori_loop(0, b + 1, body, jnp.zeros((8, GROUP), F32))
        total = lax.fori_loop(4, 4 + 4 * h, body, total)
        inverse = 1.0 / jnp.sum(total, axis=0, keepdims=True)
        stat[b] = jnp.broadcast_to(inverse, (8, GROUP))
        ust[b] = (ust[b].astype(F32) * inverse).astype(BF16)

    def split(term, own, send, rows):
        first, second = term[:128], term[128:]
        own[rows, :] = jnp.where(c == 0, first, second)
        send[rows, :] = jnp.where(c == 0, second, first).astype(BF16)

    def remote_terms(product, right, own, send):
        def body(j, carry):
            term = product(ebuf[0, aligned(j + 4, CHUNK), :], right[0])
            for b in range(1, 4):
                term += product(ebuf[b, aligned(j + 4, CHUNK), :], right[b])
            split(term, own, send, aligned(j, 128))
            return carry

        lax.fori_loop(0, 4, body, 0)

    def own_terms(product, right, own, send):
        for j in range(4):
            term = product(ebuf[j, j * CHUNK : (j + 1) * CHUNK, :], right[j])
            for b in range(j + 1, 4):
                term += product(ebuf[b, j * CHUNK : (j + 1) * CHUNK, :], right[b])
            split(term, own, send, slice(j * 128, j * 128 + 128))

    dvxs = rc(dvsend.at[1], dvsib.at[1], sib)
    dvos = rc(dvsend.at[0], dvsib.at[0], sib)
    forward_w(lower, 0)
    block_rows = [slice(b * 128, b * 128 + 128) for b in range(4)]
    dvx = [rc(dvcs.at[r], dvcr.at[r], zdev(8)) for r in block_rows]

    @pl.when(upper)
    def _():
        remote_terms(nt, ust, dvown.at[1], dvsend.at[1])
        dvxs.start()

    own_terms(nt, ust, dvown.at[0], dvsend.at[0])
    go(dvos)
    forward_w(lower, 1)

    @pl.when(upper)
    def _():
        dvxs.wait_recv()
        dvcs[...] = (dvown[1] + dvsib[1].astype(F32)).astype(BF16)
        for copy in dvx:
            copy.start()

    my_head = aligned(y, 128)
    dvb = [
        [rc(dvfull.at[r, my_head], dvfull.at[r, my_head], ydev(d)) for d in range(1, 4)]
        for r in block_rows
    ]

    dvos.wait_recv()

    @pl.when(upper)
    def _():
        dvfull[:, my_head] = (dvown[0] + dvsib[0].astype(F32)).astype(BF16)
        for copies in dvb:
            for copy in copies:
                copy.start()
        for d in range(4):
            vx[d].wait_recv()
        vxs.start()
        vxs.wait_recv()
        for j in range(4):
            vt[1, :, j * CHUNK : (j + 1) * CHUNK] = kchunk(vbuf, 1, j).T

    forward_w(upper, 0)

    vsib.wait_recv()
    for b in range(4):
        vt[0, :, b * CHUNK : (b + 1) * CHUNK] = kchunk(vbuf, 0, b).T

    def by_keys(t, b):
        def far(_, total):
            return total + nn(t[1], ebuf[b, 1024:2048, :])

        near = nn(t[0, :, : (b + 1) * CHUNK], ebuf[b, : (b + 1) * CHUNK, :])
        return lax.fori_loop(0, h, far, near)

    for b in range(4):
        out = by_keys(vt, b)
        delta = jnp.sum(ust[b].astype(F32) * out, axis=0, keepdims=True) * stat[b, 0:1, :]

        def grads(j, carry):
            dp = nn(kchunk(vbuf, j // 4, lax.rem(j, 4)), ust[b])
            e = ebuf[b, aligned(j, CHUNK), :].astype(F32)
            ebuf[b, aligned(j, CHUNK), :] = (e * (dp - delta)).astype(BF16)
            return carry

        lax.fori_loop(0, b + 1, grads, 0)
        lax.fori_loop(4, 4 + 4 * h, grads, 0)

    dkxs = rc(dksend.at[1], dksib.at[1], sib)
    dkos = rc(dksend.at[0], dksib.at[0], sib)
    dkx = rc(dkcs, dkcr, zdev(8))

    @pl.when(upper)
    def _():
        remote_terms(nn, qs, dkown.at[1], dksend.at[1])
        dkxs.start()

    own_terms(nn, qs, dkown.at[0], dksend.at[0])
    go(dkos)

    forward_w(lower, 2)
    forward_w(upper, 1)

    def weight_grad():
        for copy in nc:
            copy.wait_recv()
        for copy in own_n:
            copy.wait()
        for copies in dvb:
            for copy in copies:
                copy.wait_recv()
        for r in (1, 0):
            rsend[r] = tn(nbuf[r, :, aligned(1 - c, CHUNK)], dvfull[...]).astype(BF16)
            rs[r].start()
        for r in (1, 0):
            rown = tn(nbuf[r, :, aligned(c, CHUNK)], dvfull[...])
            rs[r].wait_recv()
            total = (rown + rsib[r].astype(F32)).astype(BF16)
            for p in range(8):
                row = pl.multiple_of(column_blocks[r] * 16 + p // 4 * 32, 32)
                rfull[p % 4, pl.ds(row, 32), :] = total[p * 32 : p * 32 + 32]
            for copy in z1[r]:
                copy.start()

    rs = [rc(rsend.at[r], rsib.at[r], sib) for r in range(2)]
    za, zb = z // 4, lax.rem(z, 4)

    def group_dev(d):
        t = za * 4 + lax.rem(zb + d, 4)
        return {"dp": lax.rem(t, 8)}

    z_rows = [pl.ds(pl.multiple_of(column_blocks[r] * 16, 64), 64) for r in range(2)]
    z1 = [
        [
            rc(
                rfull.at[lax.rem(zb + d, 4), z_rows[r]],
                z1recv.at[d - 1, z_rows[r]],
                group_dev(d),
            )
            for d in range(1, 4)
        ]
        for r in range(2)
    ]

    for b in range(4):
        total = by_keys(kt, b)
        total = total * FACTOR
        for hd in range(4):
            cols = slice(hd * 128, hd * 128 + 128)
            dqs[b, :, cols] = total[:, cols].T.astype(BF16)
    dqc = [rc(dqs.at[ys[d]], dq_o.at[:, my_group], ydev(d)) for d in range(1, 4)]
    for copy in dqc:
        go(copy)
    out_dq = lc(dqs.at[y], dq_o.at[:, my_group])
    out_dq.start()

    @pl.when(upper)
    def _():
        for copy in dvx:
            copy.wait_send()
        dkxs.wait_recv()
        dkcs[...] = ((dkown[1] + dksib[1].astype(F32)) * FACTOR).astype(BF16)
        dkx.start()

    @pl.when(upper)
    def _():
        weight_grad()

    dkos.wait_recv()
    dkc = [
        rc(dkfin.at[aligned(ys[d], 128)], dk_o.at[:, my_head], ydev(d)) for d in range(1, 4)
    ]

    out_dk = lc(dkfin.at[my_rows], dk_o.at[:, my_head])

    def send_dk():
        for copy in dkc:
            copy.start()
        out_dk.start()

    @pl.when(upper)
    def _():
        dkfin[...] = ((dkown[0] + dksib[0].astype(F32)) * FACTOR).astype(BF16)
        send_dk()

    @pl.when(lower)
    def _():
        start_w()
        for b in range(4):
            dvx[b].wait_recv()
            r = block_rows[b]
            dvfull[r, my_head] = (
                dvown[0, r, :] + dvsib[0, r, :].astype(F32) + dvcr[r, :].astype(F32)
            ).astype(BF16)
            for copy in dvb[b]:
                copy.start()
        weight_grad()

    forward_w(upper, 2)
    @pl.when(jnp.logical_or(i == 3, i == 4))
    def _():
        w_first[0].wait_recv()

    ws2 = rc(wbuf.at[1, c], wbuf.at[1, c], sib)
    go(ws2)
    def z2copy(target, slot):
        dev = {"dp": target % 2 * 4 + zb, "seq": target // 2 * 8 + y * 2 + c}
        return rc(tfull.at[aligned(target, 32)], z2recv.at[slot], dev)

    other = [(1 - h) * 2 + lax.rem(za + e, 2) for e in range(2)]
    near = za + 1 - 2 * lax.rem(za, 2)
    z2 = [[z2copy(near, 0)], [z2copy(other[0], 1), z2copy(other[1], 2)]]
    for r in (1, 0):
        for copy in z1[r]:
            copy.wait_recv()
        total = rfull[zb, z_rows[r], :].astype(F32)
        for d in range(3):
            total += z1recv[d, z_rows[r], :].astype(F32)
        tfull[z_rows[r], :] = total.astype(BF16)
        for copy in z2[r]:
            go(copy)

    wsib.wait_recv()
    own_w.wait()
    ws2.wait_recv()
    for r in range(2):
        for cc in range(2):
            gns[r, :, cc * CHUNK : (cc + 1) * CHUNK] = nt(dvfull[...], wbuf[r, cc]).astype(BF16)
    gc = []
    out_gn = []
    for r in range(2):
        cols = aligned(column_blocks[r] + y, GROUP)
        for d in range(1, 4):
            copy = rc(gns.at[r, aligned(ys[d], 128)], gn_o.at[:, cols], ydev(d))
            gc.append(copy)
            go(copy)
        out_gn.append(lc(gns.at[r, my_rows], gn_o.at[:, cols]))
        out_gn[r].start()

    my_piece = aligned(i, 32)
    total = tfull[aligned(za, 32), :].astype(F32)
    for copy in z2[0] + z2[1]:
        copy.wait_recv()
    for d in range(3):
        total += z2recv[d].astype(F32)
    zfin[my_piece, :] = total.astype(BF16)
    far_piece = aligned(lax.rem(i + 4, 8), 32)
    p1 = rc(zfin.at[my_piece], zfin.at[my_piece], {"dp": lax.rem(i + 4, 8)})
    go(p1)
    pc = [rc(zfin.at[my_piece], dw_o.at[my_piece], group_dev(d)) for d in range(1, 4)]
    for copy in pc:
        go(copy)
    p1.wait_recv()
    pf = [rc(zfin.at[far_piece], dw_o.at[far_piece], group_dev(d)) for d in range(1, 4)]
    for copy in pf:
        go(copy)
    out_dw = [lc(zfin.at[p], dw_o.at[p]) for p in (my_piece, far_piece)]
    for copy in out_dw:
        copy.start()
    @pl.when(lower)
    def _():
        dkx.wait_recv()
        dkfin[...] = (
            (dkown[0] + dksib[0].astype(F32)) * FACTOR + dkcr[...].astype(F32)
        ).astype(BF16)
        send_dk()

    for copy in pc + pf:
        copy.wait_recv()

    for copy in [out_dq, out_dk] + out_dw + out_gn:
        copy.wait()
    for copy in dqc + dkc + gc:
        copy.wait_recv()
    for copy in started + dkc + rs + [copy for copies in dvb + z1 for copy in copies]:
        copy.wait_send()

    @pl.when(lower)
    def _():
        for copy in vx:
            copy.wait_send()

    @pl.when(upper)
    def _():
        for copy in kxs + [vxs, dvxs, dkxs, dkx]:
            copy.wait_send()

    @pl.when(jnp.logical_or(first_up, first_down))
    def _():
        w_first[0].wait_send()

    @pl.when(jnp.logical_and(i != 3, i != 4))
    def _():
        w_next[0].wait_send()


def local(queries, keys, values, grad_next, normed, value_weight):
    anywhere = pl.BlockSpec(memory_space=pl.ANY)

    def buf(*shape, dtype=BF16):
        return pltpu.VMEM(shape, dtype)

    count = 100
    dq, dk, gn, dw = pl.pallas_call(
        kernel,
        out_shape=(
            jax.ShapeDtypeStruct((128, 2048), BF16),
            jax.ShapeDtypeStruct((128, 512), BF16),
            jax.ShapeDtypeStruct((128, 4096), BF16),
            jax.ShapeDtypeStruct((256, 512), BF16),
        ),
        in_specs=[anywhere] * 6,
        out_specs=(anywhere,) * 4,
        scratch_shapes=[
            buf(2, 2, 512, 128),
            buf(2, 2, 512, 128),
            buf(4, 128, GROUP),
            buf(4, 128, GROUP),
            buf(2, 512, GROUP),
            buf(2, 2, 256, 512),
            buf(4, 2048, GROUP, dtype=F32),
            buf(4, 2048, GROUP),
            buf(4, GROUP, HEAD),
            buf(4, HEAD, GROUP),
            buf(2, HEAD, 1024),
            buf(2, HEAD, 1024),
            buf(4, 8, GROUP, dtype=F32),
            buf(2, 512, 128),
            buf(2, 512, 128, dtype=F32),
            buf(2, 512, 128),
            buf(512, 128),
            buf(512, 128),
            buf(2, 512, 128),
            buf(2, 512, 128, dtype=F32),
            buf(2, 512, 128),
            buf(512, 128),
            buf(512, 128),
            buf(512, 512),
            buf(512, 128),
            buf(4, 128, GROUP),
            buf(2, 256, 512),
            buf(2, 256, 512),
            buf(4, 128, 512),
            buf(3, 128, 512),
            buf(128, 512),
            buf(3, 32, 512),
            buf(256, 512),
            buf(2, 512, GROUP),
            pltpu.SemaphoreType.DMA((count,)),
            pltpu.SemaphoreType.DMA((count,)),
            pltpu.SemaphoreType.DMA((16,)),
        ],
        compiler_params=pltpu.CompilerParams(
            collective_id=0, has_side_effects=True, vmem_limit_bytes=60 * 1024 * 1024
        ),
        cost_estimate=pl.CostEstimate(
            flops=6_000_000_000, bytes_accessed=5_000_000, transcendentals=3_000_000
        ),
    )(queries[0, 0], keys[0, 0], values[0, 0], grad_next[0, 0], normed[0, 0], value_weight[0])
    return dq[None, None], dk[None, None], gn[None, None], dw.astype(F32)[None]


def solution(mesh):
    placed = (
        P("pipe", "dp", "seq", None),
        P("pipe", "dp", "seq", None),
        P("pipe", "dp", "seq", None),
        P("pipe", "dp", "seq", None),
        P("pipe", "dp", "seq", None),
        P("pipe", "seq", None),
    )
    return jax.shard_map(
        local,
        mesh=mesh,
        in_specs=placed,
        out_specs=(
            P("pipe", "dp", "seq", None),
            P("pipe", "dp", "seq", None),
            P("pipe", "dp", "seq", None),
            P("pipe", "seq", None),
        ),
        check_vma=False,
    )
```
